128 devices in a mesh: seq: 16 (over x_lo, z, core), chan: 8 (over y, x_hi).
Axes of the slice: x: 4 (x_hi: 2, x_lo: 2; x = x_hi * 2 + x_lo), y: 4, z: 4, core: 2. Of those that a mesh axis runs over, the one named last changes fastest.
Arguments:
- tokens: bfloat16 [8192, 4096], P('seq', 'chan'), may hold values from -6 to 6
- in_weight: bfloat16 [4096, 3, 4096], P(None, None, 'chan'), may hold values from -0.09375 to 0.09375
- short_weight: float32 [3, 3, 4096], P(None, None, 'chan'), may hold values from -3 to 3
- long_filter: float32 [8192, 4096], P('seq', 'chan'), may hold values from -0.0625 to 0.0625
- skip_gain: float32 [4096], P('chan'), may hold values from -4 to 4
- out_weight: bfloat16 [4096, 4096], P('chan'), may hold values from -0.125 to 0.125
Outputs:
- mixed: bfloat16 [8192, 4096], P('seq', 'chan')
The draws below stay inside these ranges and needn't reach their ends.
All inputs are finite; a program needn't handle non-finite values.
Results may differ from the reference program's by a relative error of at most 0.019.
Values may be sent and summed in bfloat16 or wider, within the bound.
No kernel may reach another device: no remote copies, remote signals or barrier semaphores. Data moves between devices by JAX's collectives and lax.ppermute only.
A program may use at most 128 MiB of HBM per device.

```python
import jax
import jax.numpy as jnp
from jax import lax

D = 4096
L = 8192


def with_spikes(values, stream_key, source, target, shards_of, factor):
    owner, partner = [(jnp.arange(values.shape[position]) // (values.shape[position] // shards_of)).reshape([-1 if axis == position else 1 for axis in range(values.ndim)]) for position in (source, target)]
    chosen = jax.random.permutation(stream_key, shards_of)[partner]
    strong = (owner == chosen) | (owner == (partner + shards_of // 2) % shards_of)
    return jnp.where(strong, factor * values, values)


def steps_of(stream_key, extent, pieces, low, high):
    loudness = 1.0
    for axis_at, shards_of in pieces:
        heights = jax.random.uniform(jax.random.fold_in(jax.random.fold_in(stream_key, 6), axis_at), (shards_of,), jnp.float32, low / len(pieces), high / len(pieces))
        loudness = loudness * jnp.repeat(jnp.exp(heights), extent[axis_at] // shards_of).reshape((-1,) + (1,) * (len(extent) - 1 - axis_at))
    return loudness


def bell_draw(own_key, dims, width, limit, cuts=(), kind=jnp.bfloat16):
    gain = steps_of(own_key, dims, cuts, -0.22, 0.18) if cuts else 1.0
    result = jax.random.normal(own_key, dims, jnp.float32) * width * gain
    return jnp.minimum(jnp.maximum(result, -limit), limit).astype(kind)


def bell_draw_with(key, shape, deviation, most, cuts, heavy, kind=jnp.bfloat16):
    result = deviation * jax.random.normal(key, shape, jnp.float32)
    if cuts:
        result = result * steps_of(key, shape, cuts, -0.22, 0.18)
    return jnp.clip(with_spikes(result, jax.random.fold_in(key, 3), *heavy), -most, most).astype(kind)


def setup_inputs(seed: int = 0) -> dict:
    key_of = jax.random.split(jax.random.key(seed), 7)
    tokens = bell_draw(key_of[0], (L, D), 1.0, 6.0, ((0, 16), (1, 8)))
    in_weight = bell_draw(key_of[1], (D, 3, D), D ** -0.5, 0.09375, ((2, 8),))
    short_weight = bell_draw(key_of[2], (3, 3, D), 0.6, 3.0, ((2, 8),), jnp.float32)
    long_filter = bell_draw(key_of[3], (L, D), L ** -0.5, 0.0625, ((0, 16), (1, 8)), jnp.float32)
    skip_gain = bell_draw(key_of[4], (D,), 1.0, 4.0, ((0, 8),), jnp.float32)
    out_weight = bell_draw_with(key_of[5], (D, D), D ** -0.5, 0.125, ((0, 8),), (0, 1, 8, 2.0))
    return {"tokens": tokens, "in_weight": in_weight, "short_weight": short_weight, "long_filter": long_filter, "skip_gain": skip_gain, "out_weight": out_weight}


def reference(tokens, in_weight, short_weight, long_filter, skip_gain, out_weight):
    proj = jnp.dot(tokens, in_weight.reshape(D, 3 * D), preferred_element_type=jnp.float32)
    proj = proj.astype(jnp.bfloat16).astype(jnp.float32).reshape(L, 3, D)
    padded = jnp.pad(proj, ((2, 0), (0, 0), (0, 0)))
    short = short_weight[0] * padded[0:L] + short_weight[1] * padded[1:L + 1] + short_weight[2] * padded[2:L + 2]
    gate_out = short[:, 0, :]
    gate_in = short[:, 1, :]
    value = short[:, 2, :]
    signal = value * gate_in
    block = min(D, 512)
    count = D // block
    sig_blocks = jnp.transpose(signal.reshape(L, count, block), (1, 0, 2))
    fil_blocks = jnp.transpose(long_filter.reshape(L, count, block), (1, 0, 2))

    def convolve(pair):
        sig_part, fil_part = pair
        spectrum = jnp.fft.rfft(sig_part, n=2 * L, axis=0) * jnp.fft.rfft(fil_part, n=2 * L, axis=0)
        return jnp.fft.irfft(spectrum, n=2 * L, axis=0)[:L].astype(signal.dtype)

    conv = lax.map(convolve, (sig_blocks, fil_blocks))
    conv = jnp.transpose(conv, (1, 0, 2)).reshape(L, D)
    conv = conv + skip_gain * signal
    gated = (conv * gate_out).astype(jnp.bfloat16)
    return jnp.dot(gated, out_weight, preferred_element_type=jnp.float32).astype(jnp.bfloat16)
```

```python
import functools

import numpy as np
import jax
import jax.numpy as jnp
import ml_dtypes
from jax import lax
from jax.experimental import pallas as pl
from jax.experimental.pallas import tpu as pltpu
from jax.sharding import PartitionSpec as P

K1 = 72
GROUP = 8


def fourier_tables(seqs, rows):
    total = 2 * seqs * rows
    fine = 128
    coarse = total // fine
    half = coarse // 2
    per = rows // fine
    n1 = (np.arange(seqs)[None, :] * per + np.arange(per)[:, None]).reshape(-1)
    k1 = np.arange(half + 1)
    ang = 2 * np.pi * ((k1[:, None] * n1[None, :]) % coarse) / coarse
    pad = ((0, K1 - half - 1), (0, 0))
    first = np.concatenate([np.pad(np.cos(ang), pad), np.pad(-np.sin(ang), pad)])
    weight = np.where((k1 == 0) | (k1 == half), 1.0, 2.0)[:, None]
    last = np.concatenate([np.pad(weight * np.cos(ang), pad), np.pad(-weight * np.sin(ang), pad)]).T
    n2 = np.arange(fine)
    tw = 2 * np.pi * (k1[:, None] * n2[None, :]) / total
    tw_cos, tw_sin = np.pad(np.cos(tw), pad), np.pad(np.sin(tw), pad)
    ang2 = 2 * np.pi * ((n2[:, None] * n2[None, :]) % fine) / fine
    c, s = np.cos(ang2), np.sin(ang2)
    forward = np.block([[c, -s], [s, c]])
    backward = np.block([[c, s], [-s, c]])
    bf = ml_dtypes.bfloat16
    twiddle = np.stack([tw_cos, tw_sin]).astype(np.float32)
    return first.astype(bf), twiddle, forward.astype(bf), backward.astype(bf), last.astype(bf)


def spectrum_of(xs, base, seqs, chans, first, tw, forward):
    cols = []
    for i in range(GROUP):
        cols.append(jnp.concatenate([xs[p, pl.ds(base + i, seqs, stride=chans), :] for p in range(xs.shape[0])], axis=0))
    x = jnp.concatenate(cols, axis=1).astype(jnp.bfloat16)
    s = jnp.dot(first[...], x, preferred_element_type=jnp.float32)
    tc, ts = tw[0], tw[1]
    z = []
    for i in range(GROUP):
        re, im = s[:K1, i * 128:(i + 1) * 128], s[K1:, i * 128:(i + 1) * 128]
        z.append(jnp.concatenate([re * tc + im * ts, im * tc - re * ts], axis=1))
    z = jnp.concatenate(z, axis=0).astype(jnp.bfloat16)
    return jnp.dot(z, forward[...], preferred_element_type=jnp.float32)


def filter_kernel(seqs, chans, x_ref, first, tw, forward, out, xs):
    for p in range(xs.shape[0]):
        xs[p] = x_ref[:, p * 128:(p + 1) * 128].astype(jnp.float32)
    @pl.loop(0, chans // GROUP)
    def _(g):
        q = spectrum_of(xs, g * GROUP, seqs, chans, first, tw, forward)
        out[pl.ds(pl.multiple_of(g * (GROUP * K1), GROUP * K1), GROUP * K1), :] = q


def conv_kernel(seqs, chans, scale, x_ref, h_ref, first, tw, forward, backward, last, out, xs, ys):
    for p in range(xs.shape[0]):
        xs[p] = x_ref[:, p * 128:(p + 1) * 128].astype(jnp.float32)
    @pl.loop(0, chans // GROUP)
    def _(g):
        q = spectrum_of(xs, g * GROUP, seqs, chans, first, tw, forward)
        h = h_ref[pl.ds(pl.multiple_of(g * (GROUP * K1), GROUP * K1), GROUP * K1), :]
        qr, qi, hr, hi = q[:, :128], q[:, 128:], h[:, :128], h[:, 128:]
        p = jnp.concatenate([qr * hr - qi * hi, qr * hi + qi * hr], axis=1).astype(jnp.bfloat16)
        u = jnp.dot(p, backward[...], preferred_element_type=jnp.float32)
        tc, ts = tw[0] * scale, tw[1] * scale
        v = []
        for i in range(GROUP):
            re, im = u[i * K1:(i + 1) * K1, :128], u[i * K1:(i + 1) * K1, 128:]
            v.append(jnp.concatenate([re * tc - im * ts, im * tc + re * ts], axis=0))
        v = jnp.concatenate(v, axis=1).astype(jnp.bfloat16)
        y = jnp.dot(last[...], v, preferred_element_type=jnp.float32)
        for i in range(GROUP):
            yi = y[:, i * 128:(i + 1) * 128]
            for p in range(ys.shape[0]):
                ys[p, pl.ds(g * GROUP + i, seqs, stride=chans), :] = yi[p * seqs:(p + 1) * seqs]
    for p in range(ys.shape[0]):
        out[:, p * 128:(p + 1) * 128] = ys[p].astype(jnp.bfloat16)


def whole():
    return pl.BlockSpec(memory_space=pltpu.VMEM)

VM = 56 * 1024 * 1024

def filter_spectrum(x, tables, seqs):
    rows = x.shape[1]
    chans = x.shape[0] // seqs
    first, tw, forward, _, _ = tables
    return pl.pallas_call(
        functools.partial(filter_kernel, seqs, chans),
        out_shape=jax.ShapeDtypeStruct((chans * K1, 256), jnp.float32),
        in_specs=[whole()] * 4, out_specs=whole(),
        scratch_shapes=[pltpu.VMEM((x.shape[1] // 128, x.shape[0], 128), jnp.float32)],
        compiler_params=pltpu.CompilerParams(vmem_limit_bytes=VM),
        name="filter_spectrum",
        cost_estimate=pl.CostEstimate(flops=4_000_000_000, bytes_accessed=4_000_000, transcendentals=0),
    )(x, first, tw, forward)


def convolve(x, spec, tables, seqs):
    rows = x.shape[1]
    chans = x.shape[0] // seqs
    first, tw, forward, backward, last = tables
    return pl.pallas_call(
        functools.partial(conv_kernel, seqs, chans, 1.0 / (2 * seqs * rows)),
        out_shape=jax.ShapeDtypeStruct(x.shape, jnp.bfloat16),
        in_specs=[whole()] * 7, out_specs=whole(),
        scratch_shapes=[pltpu.VMEM((x.shape[1] // 128, x.shape[0], 128), jnp.float32)] * 2,
        compiler_params=pltpu.CompilerParams(vmem_limit_bytes=VM),
        name="convolve",
        cost_estimate=pl.CostEstimate(flops=5_000_000_000, bytes_accessed=4_000_000, transcendentals=0),
    )(x, spec, first, tw, forward, backward, last)


def shifted(array, axis, by):
    count = lax.axis_size(axis)
    pairs = [(i, i + by) for i in range(count) if 0 <= i + by < count]
    return lax.ppermute(array, axis, pairs)


def ring(array, by):
    count = lax.axis_size("chan")
    return lax.ppermute(array, "chan", [(i, (i + 2 * by) % count) for i in range(count)])


def cross(array):
    count = lax.axis_size("chan")
    return lax.ppermute(array, "chan", [(i, i ^ 1) for i in range(count)])


def params(**more):
    return pltpu.CompilerParams(vmem_limit_bytes=VM, **more)


def transpose_kernel(x_ref, out):
    out[...] = x_ref[...].T.astype(jnp.bfloat16)


def transposed(x):
    return pl.pallas_call(
        transpose_kernel,
        out_shape=jax.ShapeDtypeStruct(x.shape[::-1], jnp.bfloat16),
        in_specs=[whole()], out_specs=whole(),
        compiler_params=params(), name="transposed",
        cost_estimate=pl.CostEstimate(flops=0, bytes_accessed=6 * x.size, transcendentals=0),
    )(x)


def halo_kernel(x_ref, w_ref, out):
    out[0] = jnp.dot(x_ref[...], w_ref[0], preferred_element_type=jnp.float32).astype(jnp.bfloat16)


def halo_projection(halo, weight):
    branches, model, width = weight.shape
    rows = halo.shape[0]
    return pl.pallas_call(
        halo_kernel,
        grid=(branches,),
        out_shape=jax.ShapeDtypeStruct((branches, rows, width), jnp.bfloat16),
        in_specs=[pl.BlockSpec((rows, model), lambda j: (0, 0)), pl.BlockSpec((1, model, width), lambda j: (j, 0, 0))],
        out_specs=pl.BlockSpec((1, rows, width), lambda j: (j, 0, 0)),
        compiler_params=params(), name="halo_projection",
        cost_estimate=pl.CostEstimate(flops=2 * rows * weight.size, bytes_accessed=2 * weight.size, transcendentals=0),
    )(halo, weight)


def round_kernel(pieces, has_acc, owners, *refs):
    refs = list(refs)
    acc = refs.pop(0)[0] if has_acc else None
    blocks = [[refs.pop(0)[...] for _ in range(n)] for n in pieces]
    weights = [refs.pop(0) for _ in pieces]
    out = refs[0]
    for block, weight in zip(blocks, weights):
        block = block[0] if len(block) == 1 else jnp.concatenate(block, axis=0)
        term = jnp.dot(block, weight[0], preferred_element_type=jnp.float32)
        acc = term if acc is None else acc + term
    out[0] = acc


def project_round(acc, blocks, owners, weight):
    branches, _, width = weight.shape
    rows = sum(b.shape[0] for b in blocks[0])
    depth = blocks[0][0].shape[1]
    acc_spec = pl.BlockSpec((1, rows, width), lambda j, o: (j, 0, 0))
    specs = [acc_spec] if acc is not None else []
    flat = [p for b in blocks for p in b]
    specs += [pl.BlockSpec(p.shape, lambda j, o: (0, 0)) for p in flat]
    specs += [pl.BlockSpec((1, depth, width), lambda j, o, k=k: (j, o[k], 0)) for k in range(len(blocks))]
    args = ([acc] if acc is not None else []) + flat + [weight] * len(blocks)
    return pl.pallas_call(
        functools.partial(round_kernel, [len(b) for b in blocks], acc is not None),
        out_shape=jax.ShapeDtypeStruct((branches, rows, width), jnp.float32),
        grid_spec=pltpu.PrefetchScalarGridSpec(num_scalar_prefetch=1, grid=(branches,), in_specs=specs, out_specs=acc_spec),
        compiler_params=params(), name="project_round",
        cost_estimate=pl.CostEstimate(flops=2 * len(blocks) * rows * depth * branches * width, bytes_accessed=2 * len(blocks) * depth * branches * width, transcendentals=0),
    )(owners, *args)


def signal_kernel(owners, acc, lo, hi, weight, halo, taps, signal_t, signal, gate_out):
    rows = acc.shape[1]
    block = jnp.concatenate([lo[...], hi[...]], axis=0)
    short = []
    for j in range(3):
        proj = acc[j] + jnp.dot(block, weight[j], preferred_element_type=jnp.float32)
        proj = proj.astype(jnp.bfloat16).astype(jnp.float32)
        ext = jnp.concatenate([halo[j].astype(jnp.float32)[8:], proj], axis=0)
        short.append(taps[0, j:j + 1] * ext[6:6 + rows] + taps[1, j:j + 1] * ext[7:7 + rows] + taps[2, j:j + 1] * proj)
    sig = short[2] * short[1]
    gate_out[...] = short[0]
    signal[...] = sig
    signal_t[...] = sig.T.astype(jnp.bfloat16)


def signal_of(acc, lo, hi, owners, weight, halo, taps):
    branches, _, width = weight.shape
    rows = acc.shape[1]
    depth = lo.shape[1]
    cols = 256
    col = lambda c, o: (0, c)
    cube = lambda c, o: (0, 0, c)
    return pl.pallas_call(
        signal_kernel,
        out_shape=(
            jax.ShapeDtypeStruct((width, rows), jnp.bfloat16),
            jax.ShapeDtypeStruct((rows, width), jnp.float32),
            jax.ShapeDtypeStruct((rows, width), jnp.float32),
        ),
        grid_spec=pltpu.PrefetchScalarGridSpec(
            num_scalar_prefetch=1, grid=(width // cols,),
            in_specs=[
                pl.BlockSpec((branches, rows, cols), cube),
                pl.BlockSpec(lo.shape, lambda c, o: (0, 0)),
                pl.BlockSpec(hi.shape, lambda c, o: (0, 0)),
                pl.BlockSpec((branches, depth, cols), lambda c, o: (0, o[0], c)),
                pl.BlockSpec((branches, halo.shape[1], cols), cube),
                pl.BlockSpec((3, branches, cols), cube),
            ],
            out_specs=[pl.BlockSpec((cols, rows), lambda c, o: (c, 0)), pl.BlockSpec((rows, cols), col), pl.BlockSpec((rows, cols), col)],
        ),
        compiler_params=params(), name="signal_of",
    )(owners, acc, lo, hi, weight, halo, taps)


def gate_kernel(owners, conv, signal, gate_out, skip, w0, w1, w2, w3, gated, o0, o1, o2, o3):
    total = conv[...].astype(jnp.float32).T + skip[...] * signal[...]
    g = (total * gate_out[...]).astype(jnp.bfloat16)
    gated[...] = g
    for w, o in ((w0, o0), (w1, o1), (w2, o2), (w3, o3)):
        o[...] = jnp.dot(g, w[...], preferred_element_type=jnp.float32).astype(jnp.bfloat16)


def gate_and_project(part, parts, conv, signal, gate_out, skip, owners, weight):
    width, rows = conv.shape
    cols = weight.shape[1] // 8
    rows //= parts
    row = lambda i, o: (part, 0)
    out = pl.BlockSpec((rows, cols), lambda i, o: (0, 0))
    return pl.pallas_call(
        gate_kernel,
        out_shape=(jax.ShapeDtypeStruct((rows, width), jnp.bfloat16),) + (jax.ShapeDtypeStruct((rows, cols), jnp.bfloat16),) * 4,
        grid_spec=pltpu.PrefetchScalarGridSpec(
            num_scalar_prefetch=1, grid=(1,),
            in_specs=[
                pl.BlockSpec((width, rows), lambda i, o: (0, part)),
                pl.BlockSpec((rows, width), row),
                pl.BlockSpec((rows, width), row),
                pl.BlockSpec((1, width), lambda i, o: (0, 0)),
            ] + [pl.BlockSpec((width, cols), lambda i, o, k=k: (0, o[k])) for k in range(4)],
            out_specs=[pl.BlockSpec((rows, width), lambda i, o: (0, 0))] + [out] * 4,
        ),
        compiler_params=params(), name="gate_and_project",
        cost_estimate=pl.CostEstimate(flops=8 * rows * width * cols, bytes_accessed=8 * width * cols, transcendentals=0),
    )(owners, conv, signal, gate_out, skip, weight, weight, weight, weight)


def out_kernel(owners, g, w0, w1, w2, w3, o0, o1, o2, o3):
    for w, o in ((w0, o0), (w1, o1), (w2, o2), (w3, o3)):
        o[...] = jnp.dot(g[...], w[...], preferred_element_type=jnp.float32).astype(jnp.bfloat16)


def project_out(gated, owners, weight):
    rows, width = gated.shape
    cols = weight.shape[1] // 8
    out = pl.BlockSpec((rows, cols), lambda i, o: (0, 0))
    return pl.pallas_call(
        out_kernel,
        out_shape=(jax.ShapeDtypeStruct((rows, cols), jnp.bfloat16),) * 4,
        grid_spec=pltpu.PrefetchScalarGridSpec(
            num_scalar_prefetch=1, grid=(1,),
            in_specs=[pl.BlockSpec((rows, width), lambda i, o: (0, 0))]
            + [pl.BlockSpec((width, cols), lambda i, o, k=k: (0, o[k])) for k in range(4)],
            out_specs=[out] * 4,
        ),
        compiler_params=params(), name="project_out",
        cost_estimate=pl.CostEstimate(flops=8 * rows * width * cols, bytes_accessed=8 * width * cols, transcendentals=0),
    )(owners, gated, weight, weight, weight, weight)


def added(*terms):
    return sum(t.astype(jnp.float32) for t in terms).astype(jnp.bfloat16)


def shards(tables, tokens, in_weight, short_weight, long_filter, skip_gain, out_weight):
    seqs = lax.axis_size("seq")
    count = lax.axis_size("chan")
    rows, width = tokens.shape
    half = rows // 2
    me = lax.axis_index("chan")
    at = lambda dy, dx: jnp.bitwise_xor((me + 2 * dy) % count, dx).astype(jnp.int32)
    ids = lambda *pairs: jnp.stack([at(dy, dx) for dy, dx in pairs])
    weight = jnp.transpose(in_weight, (1, 0, 2))

    fil = lax.all_to_all(transposed(long_filter), "seq", 0, 0, tiled=True)
    below, above, side = ring(tokens, 1), ring(tokens, -1), cross(tokens)
    side_below, side_above = ring(side, 1), ring(side, -1)
    far_lo, far_hi = ring(below[:half], 1), ring(above[half:], -1)
    side_far_lo, side_far_hi = ring(side_below[:half], 1), ring(side_above[half:], -1)
    halo = lax.all_gather(shifted(tokens[rows - 16:], "seq", 1), "chan", axis=1, tiled=True)

    spec = filter_spectrum(fil, tables, seqs)
    acc = project_round(None, [[tokens]], ids((0, 0)), weight)
    halo = halo_projection(halo, weight)
    acc = project_round(acc, [[below], [above], [side]], ids((-1, 0), (1, 0), (0, 1)), weight)
    acc = project_round(acc, [[side_below], [side_above], [far_lo, far_hi]], ids((-1, 1), (1, 1), (2, 0)), weight)
    signal_t, signal, gate_out = signal_of(acc, side_far_lo, side_far_hi, ids((2, 1)), weight, halo, short_weight)

    conv = convolve(lax.all_to_all(signal_t, "seq", 0, 0, tiled=True), spec, tables, seqs)
    conv = lax.all_to_all(conv, "seq", 0, 0, tiled=True)

    skip = skip_gain.reshape(1, width)
    near = ids((2, 0), (1, 0), (-1, 0), (0, 0))
    wide = ids((2, 1), (1, 1), (-1, 1), (0, 1))
    g_lo, *lo = gate_and_project(0, 2, conv, signal, gate_out, skip, wide, out_weight)
    g_hi, *hi = gate_and_project(1, 2, conv, signal, gate_out, skip, wide, out_weight)

    def reduced(lo, hi):
        far_lo, up_lo, down_lo, own_lo = lo
        far_hi, up_hi, down_hi, own_hi = hi
        from_lo, from_hi = ring(far_lo, 1), ring(far_hi, -1)
        here_hi, here_lo = ring(up_hi, 1), ring(down_lo, -1)
        sum_lo = ring(added(up_lo, from_lo), 1)
        sum_hi = ring(added(down_hi, from_hi), -1)
        return (own_lo, here_lo, sum_lo), (own_hi, here_hi, sum_hi)

    wide_lo, wide_hi = reduced(lo, hi)
    wide_lo, wide_hi = cross(added(*wide_lo)), cross(added(*wide_hi))
    near_lo, near_hi = reduced(project_out(g_lo, near, out_weight), project_out(g_hi, near, out_weight))
    return jnp.concatenate([added(*near_lo, wide_lo), added(*near_hi, wide_hi)], axis=0)


def solution(mesh):
    in_specs = (
        P("seq", "chan"),
        P(None, None, "chan"),
        P(None, None, "chan"),
        P("seq", "chan"),
        P("chan"),
        P("chan", None),
    )
    def run(*args):
        seqs = mesh.shape["seq"]
        tables = tuple(jnp.asarray(t) for t in fourier_tables(seqs, args[0].shape[0] // seqs))
        body = functools.partial(shards, tables)
        return jax.shard_map(body, mesh=mesh, in_specs=in_specs, out_specs=P("seq", "chan"), check_vma=False)(*args)
    return run
```

```python
import functools

import numpy as np
import jax
import jax.numpy as jnp
import ml_dtypes
from jax import lax
from jax.experimental import pallas as pl
from jax.experimental.pallas import tpu as pltpu
from jax.sharding import PartitionSpec as P

K1 = 72
GROUP = 8


def fourier_tables(seqs, rows):
    total = 2 * seqs * rows
    fine = 128
    coarse = total // fine
    half = coarse // 2
    per = rows // fine
    n1 = (np.arange(seqs)[None, :] * per + np.arange(per)[:, None]).reshape(-1)
    k1 = np.arange(half + 1)
    ang = 2 * np.pi * ((k1[:, None] * n1[None, :]) % coarse) / coarse
    pad = ((0, K1 - half - 1), (0, 0))
    first = np.concatenate([np.pad(np.cos(ang), pad), np.pad(-np.sin(ang), pad)])
    weight = np.where((k1 == 0) | (k1 == half), 1.0, 2.0)[:, None]
    last = np.concatenate([np.pad(weight * np.cos(ang), pad), np.pad(-weight * np.sin(ang), pad)]).T
    n2 = np.arange(fine)
    tw = 2 * np.pi * (k1[:, None] * n2[None, :]) / total
    tw_cos, tw_sin = np.pad(np.cos(tw), pad), np.pad(np.sin(tw), pad)
    ang2 = 2 * np.pi * ((n2[:, None] * n2[None, :]) % fine) / fine
    c, s = np.cos(ang2), np.sin(ang2)
    forward = np.block([[c, -s], [s, c]])
    backward = np.block([[c, s], [-s, c]])
    bf = ml_dtypes.bfloat16
    twiddle = np.stack([tw_cos, tw_sin]).astype(np.float32)
    return first.astype(bf), twiddle, forward.astype(bf), backward.astype(bf), last.astype(bf)


def spectrum_of(xs, base, seqs, chans, first, tw, forward):
    cols = []
    for i in range(GROUP):
        cols.append(jnp.concatenate([xs[p, pl.ds(base + i, seqs, stride=chans), :] for p in range(xs.shape[0])], axis=0))
    x = jnp.concatenate(cols, axis=1).astype(jnp.bfloat16)
    s = jnp.dot(first[...], x, preferred_element_type=jnp.float32)
    tc, ts = tw[0], tw[1]
    z = []
    for i in range(GROUP):
        re, im = s[:K1, i * 128:(i + 1) * 128], s[K1:, i * 128:(i + 1) * 128]
        z.append(jnp.concatenate([re * tc + im * ts, im * tc - re * ts], axis=1))
    z = jnp.concatenate(z, axis=0).astype(jnp.bfloat16)
    return jnp.dot(z, forward[...], preferred_element_type=jnp.float32)


def filter_kernel(seqs, chans, x_ref, first, tw, forward, out, xs):
    for p in range(xs.shape[0]):
        xs[p] = x_ref[:, p * 128:(p + 1) * 128].astype(jnp.float32)
    @pl.loop(0, chans // GROUP)
    def _(g):
        q = spectrum_of(xs, g * GROUP, seqs, chans, first, tw, forward)
        out[pl.ds(pl.multiple_of(g * (GROUP * K1), GROUP * K1), GROUP * K1), :] = q


def conv_kernel(seqs, chans, scale, x_ref, h_ref, first, tw, forward, backward, last, out, xs, ys):
    for p in range(xs.shape[0]):
        xs[p] = x_ref[:, p * 128:(p + 1) * 128].astype(jnp.float32)
    @pl.loop(0, chans // GROUP)
    def _(g):
        q = spectrum_of(xs, g * GROUP, seqs, chans, first, tw, forward)
        h = h_ref[pl.ds(pl.multiple_of(g * (GROUP * K1), GROUP * K1), GROUP * K1), :]
        qr, qi, hr, hi = q[:, :128], q[:, 128:], h[:, :128], h[:, 128:]
        p = jnp.concatenate([qr * hr - qi * hi, qr * hi + qi * hr], axis=1).astype(jnp.bfloat16)
        u = jnp.dot(p, backward[...], preferred_element_type=jnp.float32)
        tc, ts = tw[0] * scale, tw[1] * scale
        v = []
        for i in range(GROUP):
            re, im = u[i * K1:(i + 1) * K1, :128], u[i * K1:(i + 1) * K1, 128:]
            v.append(jnp.concatenate([re * tc - im * ts, im * tc + re * ts], axis=0))
        v = jnp.concatenate(v, axis=1).astype(jnp.bfloat16)
        y = jnp.dot(last[...], v, preferred_element_type=jnp.float32)
        for i in range(GROUP):
            yi = y[:, i * 128:(i + 1) * 128]
            for p in range(ys.shape[0]):
                ys[p, pl.ds(g * GROUP + i, seqs, stride=chans), :] = yi[p * seqs:(p + 1) * seqs]
    for p in range(ys.shape[0]):
        out[:, p * 128:(p + 1) * 128] = ys[p].astype(jnp.bfloat16)


def whole():
    return pl.BlockSpec(memory_space=pltpu.VMEM)

def params(mib):
    return pltpu.CompilerParams(vmem_limit_bytes=mib * 1024 * 1024)


def filter_spectrum(x, tables, seqs):
    rows = x.shape[1]
    chans = x.shape[0] // seqs
    first, tw, forward, _, _ = tables
    return pl.pallas_call(
        functools.partial(filter_kernel, seqs, chans),
        out_shape=jax.ShapeDtypeStruct((chans * K1, 256), jnp.float32),
        in_specs=[whole()] * 4, out_specs=whole(),
        scratch_shapes=[pltpu.VMEM((x.shape[1] // 128, x.shape[0], 128), jnp.float32)],
        compiler_params=params(16),
        name="filter_spectrum",
        cost_estimate=pl.CostEstimate(flops=4_000_000_000, bytes_accessed=4_000_000, transcendentals=0),
    )(x, first, tw, forward)


def convolve(x, spec, tables, seqs):
    rows = x.shape[1]
    chans = x.shape[0] // seqs
    first, tw, forward, backward, last = tables
    return pl.pallas_call(
        functools.partial(conv_kernel, seqs, chans, 1.0 / (2 * seqs * rows)),
        out_shape=jax.ShapeDtypeStruct(x.shape, jnp.bfloat16),
        in_specs=[whole()] * 7, out_specs=whole(),
        scratch_shapes=[pltpu.VMEM((x.shape[1] // 128, x.shape[0], 128), jnp.float32)] * 2,
        compiler_params=params(16),
        name="convolve",
        cost_estimate=pl.CostEstimate(flops=5_000_000_000, bytes_accessed=4_000_000, transcendentals=0),
    )(x, spec, first, tw, forward, backward, last)


def shifted(array, axis, by):
    count = lax.axis_size(axis)
    pairs = [(i, i + by) for i in range(count) if 0 <= i + by < count]
    return lax.ppermute(array, axis, pairs)


def ring(array, by):
    count = lax.axis_size("chan")
    return lax.ppermute(array, "chan", [(i, (i + 2 * by) % count) for i in range(count)])


def cross(array):
    count = lax.axis_size("chan")
    return lax.ppermute(array, "chan", [(i, i ^ 1) for i in range(count)])


def following_far(array):
    seqs, count = lax.axis_size("seq"), lax.axis_size("chan")
    pairs = [(s * count + c, (s + 1) * count + (((c + 4) % count) ^ 1)) for s in range(seqs - 1) for c in range(count)]
    return lax.ppermute(array, ("seq", "chan"), pairs)


def transpose_kernel(x_ref, out):
    out[...] = x_ref[...].T.astype(jnp.bfloat16)


def transposed(x):
    return pl.pallas_call(
        transpose_kernel,
        out_shape=jax.ShapeDtypeStruct(x.shape[::-1], jnp.bfloat16),
        in_specs=[whole()], out_specs=whole(),
        compiler_params=params(8), name="transposed",
        cost_estimate=pl.CostEstimate(flops=0, bytes_accessed=6 * x.size, transcendentals=0),
    )(x)


def round_kernel(pieces, has_acc, owners, *refs):
    refs = list(refs)
    acc = refs.pop(0)[0] if has_acc else None
    blocks = [[refs.pop(0)[...] for _ in range(n)] for n in pieces]
    weights = [refs.pop(0) for _ in pieces]
    out = refs[0]
    for block, weight in zip(blocks, weights):
        block = block[0] if len(block) == 1 else jnp.concatenate(block, axis=0)
        term = jnp.dot(block, weight[0], preferred_element_type=jnp.float32)
        acc = term if acc is None else acc + term
    out[0] = acc


def project_round(acc, blocks, owners, weight):
    branches, _, width = weight.shape
    rows = sum(b.shape[0] for b in blocks[0])
    depth = blocks[0][0].shape[1]
    acc_spec = pl.BlockSpec((1, rows, width), lambda j, o: (j, 0, 0))
    specs = [acc_spec] if acc is not None else []
    flat = [p for b in blocks for p in b]
    specs += [pl.BlockSpec(p.shape, lambda j, o: (0, 0)) for p in flat]
    specs += [pl.BlockSpec((1, depth, width), lambda j, o, k=k: (j, o[k], 0)) for k in range(len(blocks))]
    args = ([acc] if acc is not None else []) + flat + [weight] * len(blocks)
    return pl.pallas_call(
        functools.partial(round_kernel, [len(b) for b in blocks], acc is not None),
        out_shape=jax.ShapeDtypeStruct((branches, rows, width), jnp.float32),
        grid_spec=pltpu.PrefetchScalarGridSpec(num_scalar_prefetch=1, grid=(branches,), in_specs=specs, out_specs=acc_spec),
        compiler_params=params(20), name="project_round",
        cost_estimate=pl.CostEstimate(flops=2 * len(blocks) * rows * depth * branches * width, bytes_accessed=2 * len(blocks) * depth * branches * width, transcendentals=0),
    )(owners, *args)


def signal_kernel(owners, acc, lo, hi, weight, halo, halo_acc, taps, signal_t, signal, gate_out):
    rows = acc.shape[1]
    block = jnp.concatenate([lo[...], hi[...]], axis=0)
    short = []
    for j in range(3):
        proj = acc[j] + jnp.dot(block, weight[j], preferred_element_type=jnp.float32)
        proj = proj.astype(jnp.bfloat16).astype(jnp.float32)
        before = halo_acc[j] + jnp.dot(halo[...], weight[j], preferred_element_type=jnp.float32)
        before = before.astype(jnp.bfloat16).astype(jnp.float32)
        ext = jnp.concatenate([before[8:], proj], axis=0)
        short.append(taps[0, j:j + 1] * ext[6:6 + rows] + taps[1, j:j + 1] * ext[7:7 + rows] + taps[2, j:j + 1] * proj)
    sig = short[2] * short[1]
    gate_out[...] = short[0]
    signal[...] = sig
    signal_t[...] = sig.T.astype(jnp.bfloat16)


def signal_of(acc, lo, hi, owners, weight, halo, halo_acc, taps):
    branches, _, width = weight.shape
    rows = acc.shape[1]
    depth = lo.shape[1]
    cols = 256
    col = lambda c, o: (0, c)
    cube = lambda c, o: (0, 0, c)
    fixed = lambda c, o: (0, 0)
    return pl.pallas_call(
        signal_kernel,
        out_shape=(
            jax.ShapeDtypeStruct((width, rows), jnp.bfloat16),
            jax.ShapeDtypeStruct((rows, width), jnp.float32),
            jax.ShapeDtypeStruct((rows, width), jnp.float32),
        ),
        grid_spec=pltpu.PrefetchScalarGridSpec(
            num_scalar_prefetch=1, grid=(width // cols,),
            in_specs=[
                pl.BlockSpec((branches, rows, cols), cube),
                pl.BlockSpec(lo.shape, fixed),
                pl.BlockSpec(hi.shape, fixed),
                pl.BlockSpec((branches, depth, cols), lambda c, o: (0, o[0], c)),
                pl.BlockSpec(halo.shape, fixed),
                pl.BlockSpec((branches, halo_acc.shape[1], cols), cube),
                pl.BlockSpec((3, branches, cols), cube),
            ],
            out_specs=[pl.BlockSpec((cols, rows), lambda c, o: (c, 0)), pl.BlockSpec((rows, cols), col), pl.BlockSpec((rows, cols), col)],
        ),
        compiler_params=params(20), name="signal_of",
        cost_estimate=pl.CostEstimate(flops=2 * rows * depth * branches * width, bytes_accessed=16 * rows * width, transcendentals=0),
    )(owners, acc, lo, hi, weight, halo, halo_acc, taps)


def fetch(owners, k, weight, held, sems):
    cols = held.shape[2]
    start = pl.multiple_of(owners[k] * cols, cols)
    return pltpu.make_async_copy(weight.at[:, pl.ds(start, cols)], held.at[k], sems.at[k])


def gate_kernel(owners, conv, signal, gate_out, skip, weight, gated, out, held, sems):
    copy = fetch(owners, 0, weight, held, sems)
    copy.start()
    total = conv[...].astype(jnp.float32).T + skip[...] * signal[...]
    g = (total * gate_out[...]).astype(jnp.bfloat16)
    gated[...] = g
    copy.wait()
    out[...] = jnp.dot(g, held[0], preferred_element_type=jnp.float32).astype(jnp.bfloat16)


def gate_and_project(conv, signal, gate_out, skip, owners, weight, cols):
    width, rows = conv.shape
    smem = pl.BlockSpec(memory_space=pltpu.SMEM)
    return pl.pallas_call(
        gate_kernel,
        out_shape=(jax.ShapeDtypeStruct((rows, width), jnp.bfloat16), jax.ShapeDtypeStruct((rows, cols), jnp.bfloat16)),
        in_specs=[smem] + [whole()] * 4 + [pl.BlockSpec(memory_space=pl.ANY)],
        out_specs=[whole()] * 2,
        scratch_shapes=[pltpu.VMEM((1, width, cols), jnp.bfloat16), pltpu.SemaphoreType.DMA((1,))],
        compiler_params=params(16), name="gate_and_project",
        cost_estimate=pl.CostEstimate(flops=2 * rows * width * cols, bytes_accessed=12 * rows * width, transcendentals=0),
    )(owners, conv, signal, gate_out, skip, weight)


def out_kernel(count, owners, g, weight, *refs):
    outs, (held, sems) = refs[:count], refs[count:]
    copies = [fetch(owners, k, weight, held, sems) for k in range(count)]
    for copy in copies:
        copy.start()
    for k in range(count):
        copies[k].wait()
        outs[k][...] = jnp.dot(g[...], held[k], preferred_element_type=jnp.float32).astype(jnp.bfloat16)


def project_out(gated, owners, weight, cols):
    rows, width = gated.shape
    count = owners.shape[0]
    return pl.pallas_call(
        functools.partial(out_kernel, count),
        out_shape=(jax.ShapeDtypeStruct((rows, cols), jnp.bfloat16),) * count,
        in_specs=[pl.BlockSpec(memory_space=pltpu.SMEM), whole(), pl.BlockSpec(memory_space=pl.ANY)],
        out_specs=[whole()] * count,
        scratch_shapes=[pltpu.VMEM((count, width, cols), jnp.bfloat16), pltpu.SemaphoreType.DMA((count,))],
        compiler_params=params(16), name="project_out",
        cost_estimate=pl.CostEstimate(flops=2 * count * rows * width * cols, bytes_accessed=4 * count * width * cols, transcendentals=0),
    )(owners, gated, weight)


def added(*terms):
    return sum(t.astype(jnp.float32) for t in terms).astype(jnp.bfloat16)


def shards(tables, tokens, in_weight, short_weight, long_filter, skip_gain, out_weight):
    count = lax.axis_size("chan")
    rows, width = tokens.shape
    half = rows // 2
    cols = out_weight.shape[1] // count
    me = lax.axis_index("chan")
    at = lambda dy, dx: jnp.bitwise_xor((me + 2 * dy) % count, dx).astype(jnp.int32)
    ids = lambda *pairs: jnp.stack([at(dy, dx) for dy, dx in pairs])
    weight = jnp.transpose(in_weight, (1, 0, 2))
    seqs = lax.axis_size("seq")

    below, above, side = ring(tokens, 1), ring(tokens, -1), cross(tokens)
    fil = lax.all_to_all(transposed(long_filter), "seq", 0, 0, tiled=True)
    halo = following_far(tokens[rows - 16:])
    side_below, side_above, far = ring(side, 1), cross(above), ring(above, -1)
    far_lo, far_hi = ring(side_below[:half], 1), ring(side_above[half:], -1)

    spec = filter_spectrum(fil, tables, seqs)
    acc = project_round(None, [[tokens], [below], [above], [side]], ids((0, 0), (-1, 0), (1, 0), (0, 1)), weight)
    acc = project_round(acc, [[side_below], [side_above], [far]], ids((-1, 1), (1, 1), (2, 0)), weight)
    halo_acc = shifted(acc[:, rows - 16:], "seq", 1)
    signal_t, signal, gate_out = signal_of(acc, far_lo, far_hi, ids((2, 1)), weight, halo, halo_acc, short_weight)

    conv = convolve(lax.all_to_all(signal_t, "seq", 0, 0, tiled=True), spec, tables, seqs)
    conv = lax.all_to_all(conv, "seq", 0, 0, tiled=True)

    skip = skip_gain.reshape(1, width)
    gated, far_side = gate_and_project(conv, signal, gate_out, skip, ids((2, 1)), out_weight, cols)
    to_lo, to_hi = ring(far_side[:half], -1), ring(far_side[half:], 1)
    down_side, up_side, far = project_out(gated, ids((-1, 1), (1, 1), (2, 0)), out_weight, cols)
    far = ring(far, 1)
    up, down, side, own = project_out(gated, ids((1, 0), (-1, 0), (0, 1), (0, 0)), out_weight, cols)
    down = ring(down, -1)
    down_side = ring(jnp.concatenate([added(down_side[:half], to_lo), down_side[half:]], axis=0), -1)
    up_side = cross(jnp.concatenate([up_side[:half], added(up_side[half:], to_hi)], axis=0))
    side = cross(added(side, down_side))
    up = ring(added(up, far, up_side), 1)
    return added(own, down, side, up)


def solution(mesh):
    in_specs = (
        P("seq", "chan"),
        P(None, None, "chan"),
        P(None, None, "chan"),
        P("seq", "chan"),
        P("chan"),
        P("chan", None),
    )
    def run(*args):
        seqs = mesh.shape["seq"]
        tables = tuple(jnp.asarray(t) for t in fourier_tables(seqs, args[0].shape[0] // seqs))
        body = functools.partial(shards, tables)
        return jax.shard_map(body, mesh=mesh, in_specs=in_specs, out_specs=P("seq", "chan"), check_vma=False)(*args)
    return run
```

```python
import functools

import numpy as np
import jax
import jax.numpy as jnp
import ml_dtypes
from jax import lax
from jax.experimental import pallas as pl
from jax.experimental.pallas import tpu as pltpu
from jax.sharding import PartitionSpec as P

K1 = 72
GROUP = 8


def fourier_tables(seqs, rows):
    total = 2 * seqs * rows
    fine = 128
    coarse = total // fine
    half = coarse // 2
    per = rows // fine
    n1 = (np.arange(seqs)[None, :] * per + np.arange(per)[:, None]).reshape(-1)
    k1 = np.arange(half + 1)
    ang = 2 * np.pi * ((k1[:, None] * n1[None, :]) % coarse) / coarse
    pad = ((0, K1 - half - 1), (0, 0))
    first = np.concatenate([np.pad(np.cos(ang), pad), np.pad(-np.sin(ang), pad)])
    weight = np.where((k1 == 0) | (k1 == half), 1.0, 2.0)[:, None]
    last = np.concatenate([np.pad(weight * np.cos(ang), pad), np.pad(-weight * np.sin(ang), pad)]).T
    n2 = np.arange(fine)
    tw = 2 * np.pi * (k1[:, None] * n2[None, :]) / total
    tw_cos, tw_sin = np.pad(np.cos(tw), pad), np.pad(np.sin(tw), pad)
    ang2 = 2 * np.pi * ((n2[:, None] * n2[None, :]) % fine) / fine
    c, s = np.cos(ang2), np.sin(ang2)
    forward = np.block([[c, -s], [s, c]])
    backward = np.block([[c, s], [-s, c]])
    bf = ml_dtypes.bfloat16
    twiddle = np.stack([tw_cos, tw_sin]).astype(np.float32)
    return first.astype(bf), twiddle, forward.astype(bf), backward.astype(bf), last.astype(bf)


def spectrum_of(xs, base, seqs, chans, first, tw, forward):
    cols = []
    for i in range(GROUP):
        cols.append(jnp.concatenate([xs[p, pl.ds(base + i, seqs, stride=chans), :] for p in range(xs.shape[0])], axis=0))
    x = jnp.concatenate(cols, axis=1).astype(jnp.bfloat16)
    s = jnp.dot(first[...], x, preferred_element_type=jnp.float32)
    tc, ts = tw[0], tw[1]
    z = []
    for i in range(GROUP):
        re, im = s[:K1, i * 128:(i + 1) * 128], s[K1:, i * 128:(i + 1) * 128]
        z.append(jnp.concatenate([re * tc + im * ts, im * tc - re * ts], axis=1))
    z = jnp.concatenate(z, axis=0).astype(jnp.bfloat16)
    return jnp.dot(z, forward[...], preferred_element_type=jnp.float32)


def filter_kernel(seqs, chans, x_ref, first, tw, forward, out, xs, held, sems):
    for p in range(xs.shape[0]):
        xs[p] = x_ref[:, p * 128:(p + 1) * 128].astype(jnp.float32)

    @pl.loop(0, chans // GROUP)
    def _(g):
        held[g] = spectrum_of(xs, g * GROUP, seqs, chans, first, tw, forward).astype(jnp.bfloat16)
        pltpu.make_async_copy(held.at[g], out.at[g], sems.at[g]).start()

    @pl.loop(0, chans // GROUP)
    def _(g):
        pltpu.make_async_copy(held.at[g], out.at[g], sems.at[g]).wait()


def conv_kernel(seqs, chans, scale, x_ref, h_ref, first, tw, forward, backward, last, out, xs, ys, held, sems):
    for g in range(chans // GROUP):
        pltpu.make_async_copy(h_ref.at[g], held.at[g], sems.at[g]).start()
    for p in range(xs.shape[0]):
        xs[p] = x_ref[:, p * 128:(p + 1) * 128].astype(jnp.float32)

    @pl.loop(0, chans // GROUP)
    def _(g):
        q = spectrum_of(xs, g * GROUP, seqs, chans, first, tw, forward)
        pltpu.make_async_copy(h_ref.at[g], held.at[g], sems.at[g]).wait()
        h = held[g].astype(jnp.float32)
        qr, qi, hr, hi = q[:, :128], q[:, 128:], h[:, :128], h[:, 128:]
        p = jnp.concatenate([qr * hr - qi * hi, qr * hi + qi * hr], axis=1).astype(jnp.bfloat16)
        u = jnp.dot(p, backward[...], preferred_element_type=jnp.float32)
        tc, ts = tw[0] * scale, tw[1] * scale
        v = []
        for i in range(GROUP):
            re, im = u[i * K1:(i + 1) * K1, :128], u[i * K1:(i + 1) * K1, 128:]
            v.append(jnp.concatenate([re * tc - im * ts, im * tc + re * ts], axis=0))
        v = jnp.concatenate(v, axis=1).astype(jnp.bfloat16)
        y = jnp.dot(last[...], v, preferred_element_type=jnp.float32)
        for i in range(GROUP):
            yi = y[:, i * 128:(i + 1) * 128]
            for p in range(ys.shape[0]):
                ys[p, pl.ds(g * GROUP + i, seqs, stride=chans), :] = yi[p * seqs:(p + 1) * seqs]

    for p in range(ys.shape[0]):
        out[:, p * 128:(p + 1) * 128] = ys[p].astype(jnp.bfloat16)


def whole():
    return pl.BlockSpec(memory_space=pltpu.VMEM)

def params(mib):
    return pltpu.CompilerParams(vmem_limit_bytes=mib * 1024 * 1024)


def filter_spectrum(x, tables, seqs):
    chans = x.shape[0] // seqs
    first, tw, forward, _, _ = tables
    shape = (chans // GROUP, GROUP * K1, 256)
    return pl.pallas_call(
        functools.partial(filter_kernel, seqs, chans),
        out_shape=pltpu.HBM(shape, jnp.bfloat16),
        in_specs=[whole()] * 4, out_specs=in_hbm(),
        scratch_shapes=[
            pltpu.VMEM((x.shape[1] // 128, x.shape[0], 128), jnp.float32),
            pltpu.VMEM(shape, jnp.bfloat16),
            pltpu.SemaphoreType.DMA(shape[:1]),
        ],
        compiler_params=params(10),
        name="filter_spectrum",
        cost_estimate=pl.CostEstimate(flops=4_000_000_000, bytes_accessed=4_000_000, transcendentals=0),
    )(x, first, tw, forward)


def convolve(x, spec, tables, seqs):
    rows = x.shape[1]
    chans = x.shape[0] // seqs
    first, tw, forward, backward, last = tables
    return pl.pallas_call(
        functools.partial(conv_kernel, seqs, chans, 1.0 / (2 * seqs * rows)),
        out_shape=jax.ShapeDtypeStruct(x.shape, jnp.bfloat16),
        in_specs=[whole(), in_hbm()] + [whole()] * 5, out_specs=whole(),
        scratch_shapes=[pltpu.VMEM((x.shape[1] // 128, x.shape[0], 128), jnp.float32)] * 2
        + [pltpu.VMEM(spec.shape, spec.dtype), pltpu.SemaphoreType.DMA(spec.shape[:1])],
        compiler_params=params(12),
        name="convolve",
        cost_estimate=pl.CostEstimate(flops=5_000_000_000, bytes_accessed=4_000_000, transcendentals=0),
    )(x, from_hbm(spec), first, tw, forward, backward, last)


def shifted(array, axis, by):
    count = lax.axis_size(axis)
    pairs = [(i, i + by) for i in range(count) if 0 <= i + by < count]
    return lax.ppermute(array, axis, pairs)


def ring(array, by):
    count = lax.axis_size("chan")
    return lax.ppermute(array, "chan", [(i, (i + 2 * by) % count) for i in range(count)])


def cross(array):
    count = lax.axis_size("chan")
    return lax.ppermute(array, "chan", [(i, i ^ 1) for i in range(count)])


def following(array):
    seqs, count = lax.axis_size("seq"), lax.axis_size("chan")
    pairs = [(s * count + c, (s + 1) * count + (c - 2) % count) for s in range(seqs - 1) for c in range(count)]
    return lax.ppermute(array, ("seq", "chan"), pairs)


def transpose_kernel(x_ref, out):
    out[...] = x_ref[...].T.astype(jnp.bfloat16)


def transposed(x):
    return pl.pallas_call(
        transpose_kernel,
        out_shape=jax.ShapeDtypeStruct(x.shape[::-1], jnp.bfloat16),
        in_specs=[whole()], out_specs=whole(),
        compiler_params=params(8), name="transposed",
        cost_estimate=pl.CostEstimate(flops=0, bytes_accessed=6 * x.size, transcendentals=0),
    )(x)


def owner(dy, dx):
    count = lax.axis_size("chan")
    return jnp.bitwise_xor(lax.rem(lax.axis_index("chan") + 2 * (dy % (count // 2)), count), dx)


def from_hbm(array):
    return pltpu.with_memory_space_constraint(array, pltpu.HBM)


def in_hbm():
    return pl.BlockSpec(memory_space=pltpu.HBM)


def in_vmem(array):
    return pltpu.with_memory_space_constraint(array, pltpu.VMEM)


def rows_of(weight, j, place, depth):
    start = pl.multiple_of(owner(*place) * depth, depth)
    return weight[j, pl.ds(start, depth), :]


def round_kernel(places, has_acc, tail, *refs):
    refs = list(refs)
    acc = refs.pop(0) if has_acc else None
    blocks = [refs.pop(0) for _ in places]
    weight, out, *tail_out = refs
    for j in range(out.shape[0]):
        total = acc[j] if has_acc else None
        for block, place in zip(blocks, places):
            term = jnp.dot(block[...], rows_of(weight, j, place, block.shape[1]), preferred_element_type=jnp.float32)
            total = term if total is None else total + term
        out[j] = total
        if tail:
            tail_out[0][j] = total[total.shape[0] - tail:]


def project_round(acc, blocks, places, weight, tail=0):
    branches, _, width = weight.shape
    rows, depth = blocks[0].shape
    count = len(blocks)
    args = ([acc] if acc is not None else []) + blocks
    return pl.pallas_call(
        functools.partial(round_kernel, places, acc is not None, tail),
        out_shape=[jax.ShapeDtypeStruct((branches, n, width), jnp.float32) for n in ((rows, tail) if tail else (rows,))],
        in_specs=[whole()] * (len(args) + 1),
        out_specs=[whole()] * (2 if tail else 1),
        compiler_params=params(10), name="project_round",
        cost_estimate=pl.CostEstimate(flops=2 * count * rows * depth * branches * width, bytes_accessed=2 * count * depth * branches * width, transcendentals=0),
    )(*args, in_vmem(weight))


def signal_kernel(place, acc, lo, hi, halo, halo_acc, weight, taps, signal_t, signal, gate_out, sig_t, sig, gate, out_sems):
    branches, rows, width = acc.shape
    lead = halo.shape[0]
    block = jnp.concatenate([lo[...], hi[...]], axis=0)
    cols = 256
    outs = []
    for c in range(0, width, cols):
        short = []
        for j in range(branches):
            w = rows_of(weight, j, place, block.shape[1])[:, c:c + cols]
            here = acc[j, :, c:c + cols] + jnp.dot(block, w, preferred_element_type=jnp.float32)
            before = halo_acc[j, :, c:c + cols] + jnp.dot(halo[...], w, preferred_element_type=jnp.float32)
            here, before = [p.astype(jnp.bfloat16).astype(jnp.float32) for p in (here, before)]
            ext = jnp.concatenate([before, here], axis=0)
            tap = [taps[k, j:j + 1, c:c + cols] for k in range(3)]
            short.append(tap[0] * ext[lead - 2:lead - 2 + rows] + tap[1] * ext[lead - 1:lead - 1 + rows] + tap[2] * here)
        s = short[2] * short[1]
        k = c // cols
        sig_t[c:c + cols, :] = s.T.astype(jnp.bfloat16)
        sig[k] = s
        gate[k] = short[0]
        pairs = ((sig_t.at[c:c + cols, :], signal_t.at[c:c + cols, :]), (sig.at[k], signal.at[:, c:c + cols]), (gate.at[k], gate_out.at[:, c:c + cols]))
        for i, (src, dst) in enumerate(pairs):
            outs.append(pltpu.make_async_copy(src, dst, out_sems.at[i, k]))
            outs[-1].start()
    for copy in outs:
        copy.wait()


def signal_of(acc, lo, hi, halo, halo_acc, place, weight, taps):
    branches, rows, width = acc.shape
    depth = lo.shape[1]
    parts = width // 256
    return pl.pallas_call(
        functools.partial(signal_kernel, place),
        out_shape=[pltpu.HBM((width, rows), jnp.bfloat16)] + [pltpu.HBM((rows, width), jnp.float32)] * 2,
        in_specs=[whole()] * 7,
        out_specs=[in_hbm()] * 3,
        scratch_shapes=[
            pltpu.VMEM((width, rows), jnp.bfloat16),
            pltpu.VMEM((parts, rows, 256), jnp.float32),
            pltpu.VMEM((parts, rows, 256), jnp.float32),
            pltpu.SemaphoreType.DMA((3, parts)),
        ],
        compiler_params=params(12), name="signal_of",
        cost_estimate=pl.CostEstimate(flops=2 * rows * depth * branches * width, bytes_accessed=16 * rows * width, transcendentals=0),
    )(acc, lo, hi, halo, halo_acc, in_vmem(weight), taps)


def fetch_columns(weight, at, held, sem):
    cols = held.shape[1]
    start = pl.multiple_of(at * cols, cols)
    return pltpu.make_async_copy(weight.at[:, pl.ds(start, cols)], held, sem)


def gate_kernel(places, conv, signal, gate_out, skip, weight, gated, *refs):
    outs, (held, sems) = refs[:-2], refs[-2:]
    copies = [fetch_columns(weight, owner(*p), held.at[k], sems.at[k]) for k, p in enumerate(places)]
    for copy in copies:
        copy.start()
    total = conv[...].astype(jnp.float32).T + skip[...] * signal[...]
    g = (total * gate_out[...]).astype(jnp.bfloat16)
    gated[...] = g
    half = outs[0].shape[0]
    for k in range(len(places)):
        copies[k].wait()
        outs[2 * k][...] = jnp.dot(g[:half], held[k], preferred_element_type=jnp.float32).astype(jnp.bfloat16)
        outs[2 * k + 1][...] = jnp.dot(g[half:], held[k], preferred_element_type=jnp.float32).astype(jnp.bfloat16)


def gate_and_project(conv, signal, gate_out, skip, places, weight, cols):
    width, rows = conv.shape
    count = len(places)
    return pl.pallas_call(
        functools.partial(gate_kernel, places),
        out_shape=[jax.ShapeDtypeStruct((rows, width), jnp.bfloat16)] + [jax.ShapeDtypeStruct((rows // 2, cols), jnp.bfloat16)] * (2 * count),
        in_specs=[whole()] * 4 + [in_hbm()],
        out_specs=[whole()] * (1 + 2 * count),
        scratch_shapes=[pltpu.VMEM((count, width, cols), jnp.bfloat16), pltpu.SemaphoreType.DMA((count,))],
        compiler_params=params(10), name="gate_and_project",
        cost_estimate=pl.CostEstimate(flops=2 * count * rows * width * cols, bytes_accessed=12 * rows * width, transcendentals=0),
    )(conv, signal, gate_out, skip, weight)


def out_kernel(places, pieces, g, weight, *refs):
    count = len(places)
    outs, (held, sems) = list(refs[:sum(pieces)]), refs[sum(pieces):]
    copies = [fetch_columns(weight, owner(*p), held.at[k], sems.at[k]) for k, p in enumerate(places)]
    for copy in copies:
        copy.start()
    for k in range(count):
        copies[k].wait()
        for p in range(pieces[k]):
            out = outs.pop(0)
            part = out.shape[0]
            out[...] = jnp.dot(g[p * part:(p + 1) * part], held[k], preferred_element_type=jnp.float32).astype(jnp.bfloat16)


def project_out(gated, places, pieces, weight, cols):
    rows, width = gated.shape
    count = len(places)
    return pl.pallas_call(
        functools.partial(out_kernel, places, pieces),
        out_shape=[jax.ShapeDtypeStruct((rows // n, cols), jnp.bfloat16) for n in pieces for _ in range(n)],
        in_specs=[whole(), in_hbm()],
        out_specs=[whole()] * sum(pieces),
        scratch_shapes=[pltpu.VMEM((count, width, cols), jnp.bfloat16), pltpu.SemaphoreType.DMA((count,))],
        compiler_params=params(10), name="project_out",
        cost_estimate=pl.CostEstimate(flops=2 * count * rows * width * cols, bytes_accessed=4 * count * width * cols, transcendentals=0),
    )(gated, weight)


def added(*terms):
    return sum(t.astype(jnp.float32) for t in terms).astype(jnp.bfloat16)


def shards(tables, tokens, in_weight, short_weight, long_filter, skip_gain, out_weight):
    count = lax.axis_size("chan")
    seqs = lax.axis_size("seq")
    rows, width = tokens.shape
    half = rows // 2
    cols = out_weight.shape[1] // count
    weight = jnp.transpose(in_weight, (1, 0, 2))
    together = lax.optimization_barrier

    above, side, below = ring(tokens, -1), cross(tokens), ring(tokens, 1)
    above, side, below, fil = together((above, side, below, transposed(long_filter)))
    far, side_above, side_below = ring(above, -1), cross(above), ring(side, 1)
    fil = lax.all_to_all(fil, "seq", 0, 0, tiled=True)
    acc, = project_round(None, [tokens, below, above, side], [(0, 0), (-1, 0), (1, 0), (0, 1)], weight)
    far, side_above, side_below, acc = together((far, side_above, side_below, acc))
    far_hi, far_lo = ring(side_above[half:], -1), ring(side_below[:half], 1)
    halo = following(side_above[rows - 16:])
    acc, tail = project_round(acc, [side_below, side_above, far], [(-1, 1), (1, 1), (2, 0)], weight, 16)
    halo_acc = shifted(tail, "seq", 1)
    signal_t, signal, gate_out = signal_of(acc, far_lo, far_hi, halo, halo_acc, (2, 1), weight, short_weight)
    spec = filter_spectrum(fil, tables, seqs)

    conv = convolve(lax.all_to_all(signal_t, "seq", 0, 0, tiled=True), spec, tables, seqs)
    conv = lax.all_to_all(conv, "seq", 0, 0, tiled=True)

    skip = skip_gain.reshape(1, width)
    gated, far_side_lo, far_side_hi, up_side_lo, up_side_hi = gate_and_project(conv, signal, gate_out, skip, [(2, 1), (1, 1)], out_weight, cols)
    to_hi, to_lo, up_side_lo = ring(far_side_hi, 1), ring(far_side_lo, -1), cross(up_side_lo)
    down_side, far = project_out(gated, [(-1, 1), (2, 0)], (1, 1), out_weight, cols)
    up, down, side, own = project_out(gated, [(1, 0), (-1, 0), (0, 1), (0, 0)], (1, 1, 1, 1), out_weight, cols)
    to_hi, to_lo, far, up_side_lo = together((to_hi, to_lo, far, up_side_lo))
    down_side = ring(jnp.concatenate([added(down_side[:half], to_lo), down_side[half:]], axis=0), -1)
    up_side_hi = cross(added(up_side_hi, to_hi))
    far = ring(far, 1)
    down_side, down = together((down_side, down))
    side = cross(added(side, down_side))
    up = added(up, far, jnp.concatenate([up_side_lo, up_side_hi], axis=0))
    up, down = ring(up, 1), ring(down, -1)
    return added(own, down, side, up)


def solution(mesh):
    in_specs = (
        P("seq", "chan"),
        P(None, None, "chan"),
        P(None, None, "chan"),
        P("seq", "chan"),
        P("chan"),
        P("chan", None),
    )
    def run(*args):
        seqs = mesh.shape["seq"]
        tables = tuple(jnp.asarray(t) for t in fourier_tables(seqs, args[0].shape[0] // seqs))
        body = functools.partial(shards, tables)
        return jax.shard_map(body, mesh=mesh, in_specs=in_specs, out_specs=P("seq", "chan"), check_vma=False)(*args)
    return run
```

```python
import functools

import numpy as np
import jax
import jax.numpy as jnp
import ml_dtypes
from jax import lax
from jax.experimental import pallas as pl
from jax.experimental.pallas import tpu as pltpu
from jax.sharding import PartitionSpec as P

K1 = 72
GROUP = 16


def fourier_tables(seqs, rows):
    total = 2 * seqs * rows
    fine = 128
    coarse = total // fine
    half = coarse // 2
    per = rows // fine
    n1 = (np.arange(seqs)[None, :] * per + np.arange(per)[:, None]).reshape(-1)
    k1 = np.arange(half + 1)
    ang = 2 * np.pi * ((k1[:, None] * n1[None, :]) % coarse) / coarse
    pad = ((0, K1 - half - 1), (0, 0))
    first = np.concatenate([np.pad(np.cos(ang), pad), np.pad(-np.sin(ang), pad)])
    weight = np.where((k1 == 0) | (k1 == half), 1.0, 2.0)[:, None]
    last = np.concatenate([np.pad(weight * np.cos(ang), pad), np.pad(-weight * np.sin(ang), pad)]).T
    n2 = np.arange(fine)
    tw = 2 * np.pi * (k1[:, None] * n2[None, :]) / total
    tw_cos, tw_sin = np.pad(np.cos(tw), pad), np.pad(np.sin(tw), pad)
    ang2 = 2 * np.pi * ((n2[:, None] * n2[None, :]) % fine) / fine
    c, s = np.cos(ang2), np.sin(ang2)
    forward = np.block([[c, -s], [s, c]])
    backward = np.block([[c, s], [-s, c]])
    bf = ml_dtypes.bfloat16
    twiddle = np.stack([tw_cos, tw_sin]).astype(np.float32)
    return first.astype(bf), twiddle, forward.astype(bf), backward.astype(bf), last.astype(bf)


def spectrum_of(xs, base, seqs, chans, first, tw, forward):
    cols = []
    for i in range(GROUP):
        cols.append(jnp.concatenate([xs[p, pl.ds(base + i, seqs, stride=chans), :] for p in range(xs.shape[0])], axis=0))
    x = jnp.concatenate(cols, axis=1).astype(jnp.bfloat16)
    s = jnp.dot(first[...], x, preferred_element_type=jnp.float32)
    tc, ts = tw[0], tw[1]
    z = []
    for i in range(GROUP):
        re, im = s[:K1, i * 128:(i + 1) * 128], s[K1:, i * 128:(i + 1) * 128]
        z.append(jnp.concatenate([re * tc + im * ts, im * tc - re * ts], axis=1))
    z = jnp.concatenate(z, axis=0).astype(jnp.bfloat16)
    return jnp.dot(z, forward[...], preferred_element_type=jnp.float32)


def filter_kernel(seqs, chans, x_ref, first, tw, forward, out, xs, held, sems):
    for p in range(xs.shape[0]):
        xs[p] = x_ref[:, p * 128:(p + 1) * 128].astype(jnp.float32)

    @pl.loop(0, chans // GROUP)
    def _(g):
        held[g] = spectrum_of(xs, g * GROUP, seqs, chans, first, tw, forward).astype(jnp.bfloat16)
        pltpu.make_async_copy(held.at[g], out.at[g], sems.at[g]).start()

    @pl.loop(0, chans // GROUP)
    def _(g):
        pltpu.make_async_copy(held.at[g], out.at[g], sems.at[g]).wait()


def conv_kernel(seqs, chans, scale, x_ref, h_ref, first, tw, forward, backward, last, out, xs, ys, held, sems):
    for g in range(chans // GROUP):
        pltpu.make_async_copy(h_ref.at[g], held.at[g], sems.at[g]).start()
    for p in range(xs.shape[0]):
        xs[p] = x_ref[:, p * 128:(p + 1) * 128].astype(jnp.float32)

    @pl.loop(0, chans // GROUP)
    def _(g):
        q = spectrum_of(xs, g * GROUP, seqs, chans, first, tw, forward)
        pltpu.make_async_copy(h_ref.at[g], held.at[g], sems.at[g]).wait()
        h = held[g].astype(jnp.float32)
        qr, qi, hr, hi = q[:, :128], q[:, 128:], h[:, :128], h[:, 128:]
        p = jnp.concatenate([qr * hr - qi * hi, qr * hi + qi * hr], axis=1).astype(jnp.bfloat16)
        u = jnp.dot(p, backward[...], preferred_element_type=jnp.float32)
        tc, ts = tw[0] * scale, tw[1] * scale
        v = []
        for i in range(GROUP):
            re, im = u[i * K1:(i + 1) * K1, :128], u[i * K1:(i + 1) * K1, 128:]
            v.append(jnp.concatenate([re * tc - im * ts, im * tc + re * ts], axis=0))
        v = jnp.concatenate(v, axis=1).astype(jnp.bfloat16)
        y = jnp.dot(last[...], v, preferred_element_type=jnp.float32)
        for i in range(GROUP):
            yi = y[:, i * 128:(i + 1) * 128]
            for p in range(ys.shape[0]):
                ys[p, pl.ds(g * GROUP + i, seqs, stride=chans), :] = yi[p * seqs:(p + 1) * seqs]

    for p in range(ys.shape[0]):
        out[:, p * 128:(p + 1) * 128] = ys[p].astype(jnp.bfloat16)


def whole():
    return pl.BlockSpec(memory_space=pltpu.VMEM)

def params(mib):
    return pltpu.CompilerParams(vmem_limit_bytes=mib * 1024 * 1024)


def filter_spectrum(x, tables, seqs):
    chans = x.shape[0] // seqs
    first, tw, forward, _, _ = tables
    shape = (chans // GROUP, GROUP * K1, 256)
    return pl.pallas_call(
        functools.partial(filter_kernel, seqs, chans),
        out_shape=pltpu.HBM(shape, jnp.bfloat16),
        in_specs=[whole()] * 4, out_specs=in_hbm(),
        scratch_shapes=[
            pltpu.VMEM((x.shape[1] // 128, x.shape[0], 128), jnp.float32),
            pltpu.VMEM(shape, jnp.bfloat16),
            pltpu.SemaphoreType.DMA(shape[:1]),
        ],
        compiler_params=params(10),
        name="filter_spectrum",
        cost_estimate=pl.CostEstimate(flops=4_000_000_000, bytes_accessed=4_000_000, transcendentals=0),
    )(x, first, tw, forward)


def convolve(x, spec, tables, seqs):
    rows = x.shape[1]
    chans = x.shape[0] // seqs
    first, tw, forward, backward, last = tables
    return pl.pallas_call(
        functools.partial(conv_kernel, seqs, chans, 1.0 / (2 * seqs * rows)),
        out_shape=jax.ShapeDtypeStruct(x.shape, jnp.bfloat16),
        in_specs=[whole(), in_hbm()] + [whole()] * 5, out_specs=whole(),
        scratch_shapes=[pltpu.VMEM((x.shape[1] // 128, x.shape[0], 128), jnp.float32)] * 2
        + [pltpu.VMEM(spec.shape, spec.dtype), pltpu.SemaphoreType.DMA(spec.shape[:1])],
        compiler_params=params(12),
        name="convolve",
        cost_estimate=pl.CostEstimate(flops=5_000_000_000, bytes_accessed=4_000_000, transcendentals=0),
    )(x, from_hbm(spec), first, tw, forward, backward, last)


def shifted(array, axis, by):
    count = lax.axis_size(axis)
    pairs = [(i, i + by) for i in range(count) if 0 <= i + by < count]
    return lax.ppermute(array, axis, pairs)


def ring(array, by):
    count = lax.axis_size("chan")
    return lax.ppermute(array, "chan", [(i, (i + 2 * by) % count) for i in range(count)])


def cross(array):
    count = lax.axis_size("chan")
    return lax.ppermute(array, "chan", [(i, i ^ 1) for i in range(count)])


def following_far(array):
    seqs, count = lax.axis_size("seq"), lax.axis_size("chan")
    pairs = [(s * count + c, (s + 1) * count + (((c + 4) % count) ^ 1)) for s in range(seqs - 1) for c in range(count)]
    return lax.ppermute(array, ("seq", "chan"), pairs)


def transpose_kernel(x_ref, out):
    out[...] = x_ref[...].T.astype(jnp.bfloat16)


def transposed(x):
    return pl.pallas_call(
        transpose_kernel,
        out_shape=jax.ShapeDtypeStruct(x.shape[::-1], jnp.bfloat16),
        in_specs=[whole()], out_specs=whole(),
        compiler_params=params(8), name="transposed",
        cost_estimate=pl.CostEstimate(flops=0, bytes_accessed=6 * x.size, transcendentals=0),
    )(x)


def owner(dy, dx):
    count = lax.axis_size("chan")
    return jnp.bitwise_xor(lax.rem(lax.axis_index("chan") + 2 * (dy % (count // 2)), count), dx)


def from_hbm(array):
    return pltpu.with_memory_space_constraint(array, pltpu.HBM)


def in_hbm():
    return pl.BlockSpec(memory_space=pltpu.HBM)


def in_vmem(array):
    return pltpu.with_memory_space_constraint(array, pltpu.VMEM)


def rows_of(weight, j, place, depth):
    start = pl.multiple_of(owner(*place) * depth, depth)
    return weight[j, pl.ds(start, depth), :]


def round_kernel(places, has_acc, tail, *refs):
    refs = list(refs)
    acc = refs.pop(0) if has_acc else None
    blocks = [refs.pop(0) for _ in places]
    weight, out, *tail_out = refs
    for j in range(out.shape[0]):
        total = acc[j] if has_acc else None
        for block, place in zip(blocks, places):
            term = jnp.dot(block[...], rows_of(weight, j, place, block.shape[1]), preferred_element_type=jnp.float32)
            total = term if total is None else total + term
        out[j] = total
        if tail:
            tail_out[0][j] = total[total.shape[0] - tail:]


def project_round(acc, blocks, places, weight, tail=0):
    branches, _, width = weight.shape
    rows, depth = blocks[0].shape
    count = len(blocks)
    args = ([acc] if acc is not None else []) + blocks
    return pl.pallas_call(
        functools.partial(round_kernel, places, acc is not None, tail),
        out_shape=[jax.ShapeDtypeStruct((branches, n, width), jnp.float32) for n in ((rows, tail) if tail else (rows,))],
        in_specs=[whole()] * (len(args) + 1),
        out_specs=[whole()] * (2 if tail else 1),
        compiler_params=params(10), name="project_round",
        cost_estimate=pl.CostEstimate(flops=2 * count * rows * depth * branches * width, bytes_accessed=2 * count * depth * branches * width, transcendentals=0),
    )(*args, in_vmem(weight))


def fetch_rows(weight, j, at, held, sem):
    depth = held.shape[0]
    start = pl.multiple_of(at * depth, depth)
    return pltpu.make_async_copy(weight.at[j, pl.ds(start, depth)], held, sem)


def first_kernel(places, *refs):
    blocks, (weight, out, held, sems) = refs[:-4], refs[-4:]
    branches = out.shape[0]
    copies = [[fetch_rows(weight, j, owner(*p), held.at[j, k], sems.at[j, k]) for k, p in enumerate(places)] for j in range(branches)]
    for row in copies:
        for copy in row:
            copy.start()
    for j in range(branches):
        total = None
        for k in range(len(places)):
            copies[j][k].wait()
            term = jnp.dot(blocks[k][...], held[j, k], preferred_element_type=jnp.float32)
            total = term if total is None else total + term
        out[j] = total


def first_round(blocks, places, weight):
    branches, _, width = weight.shape
    rows, depth = blocks[0].shape
    count = len(blocks)
    return pl.pallas_call(
        functools.partial(first_kernel, places),
        out_shape=jax.ShapeDtypeStruct((branches, rows, width), jnp.float32),
        in_specs=[whole()] * count + [in_hbm()],
        out_specs=whole(),
        scratch_shapes=[pltpu.VMEM((branches, count, depth, width), jnp.bfloat16), pltpu.SemaphoreType.DMA((branches, count))],
        compiler_params=params(10), name="first_round",
        cost_estimate=pl.CostEstimate(flops=2 * count * rows * depth * branches * width, bytes_accessed=2 * count * depth * branches * width, transcendentals=0),
    )(*blocks, from_hbm(weight))


def signal_kernel(place, acc, lo, hi, halo, halo_acc, weight, taps, signal_t, signal, gate_out, sig_t, sig, gate, out_sems):
    branches, rows, width = acc.shape
    lead = halo.shape[0]
    block = jnp.concatenate([lo[...], hi[...]], axis=0)
    cols = 256
    outs = []
    for c in range(0, width, cols):
        short = []
        for j in range(branches):
            w = rows_of(weight, j, place, block.shape[1])[:, c:c + cols]
            here = acc[j, :, c:c + cols] + jnp.dot(block, w, preferred_element_type=jnp.float32)
            before = halo_acc[j, :, c:c + cols] + jnp.dot(halo[...], w, preferred_element_type=jnp.float32)
            here, before = [p.astype(jnp.bfloat16).astype(jnp.float32) for p in (here, before)]
            ext = jnp.concatenate([before, here], axis=0)
            tap = [taps[k, j:j + 1, c:c + cols] for k in range(3)]
            short.append(tap[0] * ext[lead - 2:lead - 2 + rows] + tap[1] * ext[lead - 1:lead - 1 + rows] + tap[2] * here)
        s = short[2] * short[1]
        k = c // cols
        sig_t[c:c + cols, :] = s.T.astype(jnp.bfloat16)
        sig[k] = s
        gate[k] = short[0]
        pairs = ((sig_t.at[c:c + cols, :], signal_t.at[c:c + cols, :]), (sig.at[k], signal.at[:, c:c + cols]), (gate.at[k], gate_out.at[:, c:c + cols]))
        for i, (src, dst) in enumerate(pairs):
            outs.append(pltpu.make_async_copy(src, dst, out_sems.at[i, k]))
            outs[-1].start()
    for copy in outs:
        copy.wait()


def signal_of(acc, lo, hi, halo, halo_acc, place, weight, taps):
    branches, rows, width = acc.shape
    depth = lo.shape[1]
    parts = width // 256
    return pl.pallas_call(
        functools.partial(signal_kernel, place),
        out_shape=[pltpu.HBM((width, rows), jnp.bfloat16)] + [pltpu.HBM((rows, width), jnp.float32)] * 2,
        in_specs=[whole()] * 7,
        out_specs=[in_hbm()] * 3,
        scratch_shapes=[
            pltpu.VMEM((width, rows), jnp.bfloat16),
            pltpu.VMEM((parts, rows, 256), jnp.float32),
            pltpu.VMEM((parts, rows, 256), jnp.float32),
            pltpu.SemaphoreType.DMA((3, parts)),
        ],
        compiler_params=params(12), name="signal_of",
        cost_estimate=pl.CostEstimate(flops=2 * rows * depth * branches * width, bytes_accessed=16 * rows * width, transcendentals=0),
    )(acc, lo, hi, halo, halo_acc, in_vmem(weight), taps)


def fetch_columns(weight, at, held, sem):
    cols = held.shape[1]
    start = pl.multiple_of(at * cols, cols)
    return pltpu.make_async_copy(weight.at[:, pl.ds(start, cols)], held, sem)


def gate_kernel(place, conv, signal, gate_out, skip, weight, gated, *refs):
    outs, (held, sem) = refs[:-2], refs[-2:]
    copy = fetch_columns(weight, owner(*place), held, sem)
    copy.start()
    total = conv[...].astype(jnp.float32).T + skip[...] * signal[...]
    g = (total * gate_out[...]).astype(jnp.bfloat16)
    gated[...] = g
    copy.wait()
    at = 0
    for out in outs:
        out[...] = jnp.dot(g[at:at + out.shape[0]], held[...], preferred_element_type=jnp.float32).astype(jnp.bfloat16)
        at += out.shape[0]


def gate_and_project(conv, signal, gate_out, skip, place, pieces, weight, cols):
    rows, width = signal.shape
    return pl.pallas_call(
        functools.partial(gate_kernel, place),
        out_shape=[jax.ShapeDtypeStruct((rows, width), jnp.bfloat16)] + [jax.ShapeDtypeStruct((n, cols), jnp.bfloat16) for n in pieces],
        in_specs=[whole()] * 4 + [in_hbm()],
        out_specs=[whole()] * (1 + len(pieces)),
        scratch_shapes=[pltpu.VMEM((width, cols), jnp.bfloat16), pltpu.SemaphoreType.DMA],
        compiler_params=params(10), name="gate_and_project",
        cost_estimate=pl.CostEstimate(flops=2 * rows * width * cols, bytes_accessed=12 * rows * width, transcendentals=0),
    )(conv, signal, gate_out, skip, weight)


def out_kernel(places, pieces, g, weight, *refs):
    count = len(places)
    outs, (held, sems) = list(refs[:sum(pieces)]), refs[sum(pieces):]
    copies = [fetch_columns(weight, owner(*p), held.at[k], sems.at[k]) for k, p in enumerate(places)]
    for copy in copies:
        copy.start()
    for k in range(count):
        copies[k].wait()
        for p in range(pieces[k]):
            out = outs.pop(0)
            part = out.shape[0]
            out[...] = jnp.dot(g[p * part:(p + 1) * part], held[k], preferred_element_type=jnp.float32).astype(jnp.bfloat16)


def project_out(gated, places, pieces, weight, cols):
    rows, width = gated.shape
    count = len(places)
    return pl.pallas_call(
        functools.partial(out_kernel, places, pieces),
        out_shape=[jax.ShapeDtypeStruct((rows // n, cols), jnp.bfloat16) for n in pieces for _ in range(n)],
        in_specs=[whole(), in_hbm()],
        out_specs=[whole()] * sum(pieces),
        scratch_shapes=[pltpu.VMEM((count, width, cols), jnp.bfloat16), pltpu.SemaphoreType.DMA((count,))],
        compiler_params=params(10), name="project_out",
        cost_estimate=pl.CostEstimate(flops=2 * count * rows * width * cols, bytes_accessed=4 * count * width * cols, transcendentals=0),
    )(gated, weight)


def thirds(rows):
    tiles = rows // 16
    return (tiles + 2) // 3 * 16, 2 * ((tiles + 2) // 3) * 16


def added(*terms):
    return sum(t.astype(jnp.float32) for t in terms).astype(jnp.bfloat16)


def shards(tables, tokens, in_weight, short_weight, long_filter, skip_gain, out_weight):
    count = lax.axis_size("chan")
    seqs = lax.axis_size("seq")
    rows, width = tokens.shape
    half = rows // 2
    cols = out_weight.shape[1] // count
    weight = jnp.transpose(in_weight, (1, 0, 2))
    together = lax.optimization_barrier

    above, side, below = ring(tokens, -1), cross(tokens), ring(tokens, 1)
    halo = following_far(tokens[rows - 16:])
    above, side, below, halo, fil = together((above, side, below, halo, transposed(long_filter)))
    far, side_above, side_below = ring(above, -1), cross(above), ring(side, 1)
    fil = lax.all_to_all(fil, "seq", 0, 0, tiled=True)
    acc = first_round([tokens, below, above, side], [(0, 0), (-1, 0), (1, 0), (0, 1)], weight)
    far, side_above, side_below, acc = together((far, side_above, side_below, acc))
    far_hi, far_lo = ring(side_above[half:], -1), ring(side_below[:half], 1)
    acc, tail = project_round(acc, [side_below, side_above, far], [(-1, 1), (1, 1), (2, 0)], weight, 16)
    halo_acc = shifted(tail, "seq", 1)
    signal_t, signal, gate_out = signal_of(acc, far_lo, far_hi, halo, halo_acc, (2, 1), weight, short_weight)
    spec = filter_spectrum(fil, tables, seqs)

    conv = convolve(lax.all_to_all(signal_t, "seq", 0, 0, tiled=True), spec, tables, seqs)
    conv = lax.all_to_all(conv, "seq", 0, 0, tiled=True)

    skip = skip_gain.reshape(1, width)
    one, two = thirds(rows)
    gated, *pieces = gate_and_project(conv, signal, gate_out, skip, (2, 1), (one, two - one, rows - two), out_weight, cols)
    to_down, to_up, to_far = ring(pieces[0], -1), ring(pieces[1], 1), cross(pieces[2])
    up_side, down_side, far = project_out(gated, [(1, 1), (-1, 1), (2, 0)], (1, 1, 1), out_weight, cols)
    up, down, side, own = project_out(gated, [(1, 0), (-1, 0), (0, 1), (0, 0)], (1, 1, 1, 1), out_weight, cols)
    down_side = ring(jnp.concatenate([added(down_side[:one], to_down), down_side[one:]], axis=0), -1)
    up_side = cross(jnp.concatenate([up_side[:one], added(up_side[one:two], to_up), up_side[two:]], axis=0))
    far = ring(jnp.concatenate([far[:two], added(far[two:], to_far)], axis=0), 1)
    down_side, down = together((down_side, down))
    side = cross(added(side, down_side))
    up = added(up, far, up_side)
    up, down = ring(up, 1), ring(down, -1)
    return added(own, down, side, up)


def solution(mesh):
    in_specs = (
        P("seq", "chan"),
        P(None, None, "chan"),
        P(None, None, "chan"),
        P("seq", "chan"),
        P("chan"),
        P("chan", None),
    )
    def run(*args):
        seqs = mesh.shape["seq"]
        tables = tuple(jnp.asarray(t) for t in fourier_tables(seqs, args[0].shape[0] // seqs))
        body = functools.partial(shards, tables)
        return jax.shard_map(body, mesh=mesh, in_specs=in_specs, out_specs=P("seq", "chan"), check_vma=False)(*args)
    return run
```

```python
import functools

import numpy as np
import jax
import jax.numpy as jnp
import ml_dtypes
from jax import lax
from jax.experimental import pallas as pl
from jax.experimental.pallas import tpu as pltpu
from jax.sharding import PartitionSpec as P

K1 = 72
GROUP = 32


def fourier_tables(seqs, rows):
    total = 2 * seqs * rows
    fine = 128
    coarse = total // fine
    half = coarse // 2
    per = rows // fine
    n1 = (np.arange(seqs)[None, :] * per + np.arange(per)[:, None]).reshape(-1)
    k1 = np.arange(half + 1)
    ang = 2 * np.pi * ((k1[:, None] * n1[None, :]) % coarse) / coarse
    pad = ((0, K1 - half - 1), (0, 0))
    first = np.concatenate([np.pad(np.cos(ang), pad), np.pad(-np.sin(ang), pad)])
    weight = np.where((k1 == 0) | (k1 == half), 1.0, 2.0)[:, None]
    last = np.concatenate([np.pad(weight * np.cos(ang), pad), np.pad(-weight * np.sin(ang), pad)]).T
    n2 = np.arange(fine)
    tw = 2 * np.pi * (k1[:, None] * n2[None, :]) / total
    tw_cos, tw_sin = np.pad(np.cos(tw), pad), np.pad(np.sin(tw), pad)
    ang2 = 2 * np.pi * ((n2[:, None] * n2[None, :]) % fine) / fine
    c, s = np.cos(ang2), np.sin(ang2)
    forward = np.block([[c, -s], [s, c]])
    backward = np.block([[c, s], [-s, c]])
    bf = ml_dtypes.bfloat16
    twiddle = np.stack([tw_cos, tw_sin]).astype(np.float32)
    return first.astype(bf), twiddle, forward.astype(bf), backward.astype(bf), last.astype(bf)


def spectrum_of(xs, base, seqs, chans, first, tw, forward):
    cols = []
    for i in range(GROUP):
        cols.append(jnp.concatenate([xs[p, pl.ds(base + i, seqs, stride=chans), :] for p in range(xs.shape[0])], axis=0))
    x = jnp.concatenate(cols, axis=1).astype(jnp.bfloat16)
    s = jnp.dot(first[...], x, preferred_element_type=jnp.float32)
    tc, ts = tw[0], tw[1]
    z = []
    for i in range(GROUP):
        re, im = s[:K1, i * 128:(i + 1) * 128], s[K1:, i * 128:(i + 1) * 128]
        z.append(jnp.concatenate([re * tc + im * ts, im * tc - re * ts], axis=1))
    z = jnp.concatenate(z, axis=0).astype(jnp.bfloat16)
    return jnp.dot(z, forward[...], preferred_element_type=jnp.float32)


def filter_kernel(seqs, chans, x_ref, first, tw, forward, out, xs, held, sems):
    for p in range(xs.shape[0]):
        xs[p] = x_ref[:, p * 128:(p + 1) * 128].astype(jnp.float32)

    @pl.loop(0, chans // GROUP)
    def _(g):
        held[g] = spectrum_of(xs, g * GROUP, seqs, chans, first, tw, forward).astype(jnp.bfloat16)
        pltpu.make_async_copy(held.at[g], out.at[g], sems.at[g]).start()

    @pl.loop(0, chans // GROUP)
    def _(g):
        pltpu.make_async_copy(held.at[g], out.at[g], sems.at[g]).wait()


def conv_kernel(seqs, chans, scale, x_ref, h_ref, first, tw, forward, backward, last, out, xs, ys, held, sems):
    for g in range(chans // GROUP):
        pltpu.make_async_copy(h_ref.at[g], held.at[g], sems.at[g]).start()
    for p in range(xs.shape[0]):
        xs[p] = x_ref[:, p * 128:(p + 1) * 128].astype(jnp.float32)

    @pl.loop(0, chans // GROUP)
    def _(g):
        q = spectrum_of(xs, g * GROUP, seqs, chans, first, tw, forward)
        pltpu.make_async_copy(h_ref.at[g], held.at[g], sems.at[g]).wait()
        h = held[g].astype(jnp.float32)
        qr, qi, hr, hi = q[:, :128], q[:, 128:], h[:, :128], h[:, 128:]
        p = jnp.concatenate([qr * hr - qi * hi, qr * hi + qi * hr], axis=1).astype(jnp.bfloat16)
        u = jnp.dot(p, backward[...], preferred_element_type=jnp.float32)
        tc, ts = tw[0] * scale, tw[1] * scale
        v = []
        for i in range(GROUP):
            re, im = u[i * K1:(i + 1) * K1, :128], u[i * K1:(i + 1) * K1, 128:]
            v.append(jnp.concatenate([re * tc - im * ts, im * tc + re * ts], axis=0))
        v = jnp.concatenate(v, axis=1).astype(jnp.bfloat16)
        y = jnp.dot(last[...], v, preferred_element_type=jnp.float32)
        for i in range(GROUP):
            yi = y[:, i * 128:(i + 1) * 128]
            for p in range(ys.shape[0]):
                ys[p, pl.ds(g * GROUP + i, seqs, stride=chans), :] = yi[p * seqs:(p + 1) * seqs]

    for p in range(ys.shape[0]):
        out[:, p * 128:(p + 1) * 128] = ys[p].astype(jnp.bfloat16)


def whole():
    return pl.BlockSpec(memory_space=pltpu.VMEM)

def params(mib):
    return pltpu.CompilerParams(vmem_limit_bytes=mib * 1024 * 1024)


def filter_spectrum(x, tables, seqs):
    chans = x.shape[0] // seqs
    first, tw, forward, _, _ = tables
    shape = (chans // GROUP, GROUP * K1, 256)
    return pl.pallas_call(
        functools.partial(filter_kernel, seqs, chans),
        out_shape=pltpu.HBM(shape, jnp.bfloat16),
        in_specs=[whole()] * 4, out_specs=in_hbm(),
        scratch_shapes=[
            pltpu.VMEM((x.shape[1] // 128, x.shape[0], 128), jnp.float32),
            pltpu.VMEM(shape, jnp.bfloat16),
            pltpu.SemaphoreType.DMA(shape[:1]),
        ],
        compiler_params=params(16),
        name="filter_spectrum",
        cost_estimate=pl.CostEstimate(flops=4_000_000_000, bytes_accessed=4_000_000, transcendentals=0),
    )(x, first, tw, forward)


def convolve(x, spec, tables, seqs):
    rows = x.shape[1]
    chans = x.shape[0] // seqs
    first, tw, forward, backward, last = tables
    return pl.pallas_call(
        functools.partial(conv_kernel, seqs, chans, 1.0 / (2 * seqs * rows)),
        out_shape=jax.ShapeDtypeStruct(x.shape, jnp.bfloat16),
        in_specs=[whole(), in_hbm()] + [whole()] * 5, out_specs=whole(),
        scratch_shapes=[pltpu.VMEM((x.shape[1] // 128, x.shape[0], 128), jnp.float32)] * 2
        + [pltpu.VMEM(spec.shape, spec.dtype), pltpu.SemaphoreType.DMA(spec.shape[:1])],
        compiler_params=params(20),
        name="convolve",
        cost_estimate=pl.CostEstimate(flops=5_000_000_000, bytes_accessed=4_000_000, transcendentals=0),
    )(x, from_hbm(spec), first, tw, forward, backward, last)


def shifted(array, axis, by):
    count = lax.axis_size(axis)
    pairs = [(i, i + by) for i in range(count) if 0 <= i + by < count]
    return lax.ppermute(array, axis, pairs)


def ring(array, by):
    count = lax.axis_size("chan")
    return lax.ppermute(array, "chan", [(i, (i + 2 * by) % count) for i in range(count)])


def cross(array):
    count = lax.axis_size("chan")
    return lax.ppermute(array, "chan", [(i, i ^ 1) for i in range(count)])


def following_far(array):
    seqs, count = lax.axis_size("seq"), lax.axis_size("chan")
    pairs = [(s * count + c, (s + 1) * count + (((c + 4) % count) ^ 1)) for s in range(seqs - 1) for c in range(count)]
    return lax.ppermute(array, ("seq", "chan"), pairs)


def transpose_kernel(x_ref, out):
    out[...] = x_ref[...].T.astype(jnp.bfloat16)


def transposed(x):
    return pl.pallas_call(
        transpose_kernel,
        out_shape=jax.ShapeDtypeStruct(x.shape[::-1], jnp.bfloat16),
        in_specs=[whole()], out_specs=whole(),
        compiler_params=params(8), name="transposed",
        cost_estimate=pl.CostEstimate(flops=0, bytes_accessed=6 * x.size, transcendentals=0),
    )(x)


def owner(dy, dx):
    count = lax.axis_size("chan")
    return jnp.bitwise_xor(lax.rem(lax.axis_index("chan") + 2 * (dy % (count // 2)), count), dx)


def from_hbm(array):
    return pltpu.with_memory_space_constraint(array, pltpu.HBM)


def in_hbm():
    return pl.BlockSpec(memory_space=pltpu.HBM)


def in_vmem(array):
    return pltpu.with_memory_space_constraint(array, pltpu.VMEM)


def rows_of(weight, j, place, depth):
    start = pl.multiple_of(owner(*place) * depth, depth)
    return weight[j, pl.ds(start, depth), :]


def round_kernel(places, has_acc, tail, *refs):
    refs = list(refs)
    acc = refs.pop(0) if has_acc else None
    blocks = [refs.pop(0) for _ in places]
    weight, out, *tail_out = refs
    for j in range(out.shape[0]):
        total = acc[j] if has_acc else None
        for block, place in zip(blocks, places):
            term = jnp.dot(block[...], rows_of(weight, j, place, block.shape[1]), preferred_element_type=jnp.float32)
            total = term if total is None else total + term
        out[j] = total
        if tail:
            tail_out[0][j] = total[total.shape[0] - tail:]


def project_round(acc, blocks, places, weight, tail=0):
    branches, _, width = weight.shape
    rows, depth = blocks[0].shape
    count = len(blocks)
    args = ([acc] if acc is not None else []) + blocks
    return pl.pallas_call(
        functools.partial(round_kernel, places, acc is not None, tail),
        out_shape=[jax.ShapeDtypeStruct((branches, n, width), jnp.float32) for n in ((rows, tail) if tail else (rows,))],
        in_specs=[whole()] * (len(args) + 1),
        out_specs=[whole()] * (2 if tail else 1),
        compiler_params=params(10), name="project_round",
        cost_estimate=pl.CostEstimate(flops=2 * count * rows * depth * branches * width, bytes_accessed=2 * count * depth * branches * width, transcendentals=0),
    )(*args, in_vmem(weight))


def fetch_rows(weight, j, at, held, sem):
    depth = held.shape[0]
    start = pl.multiple_of(at * depth, depth)
    return pltpu.make_async_copy(weight.at[j, pl.ds(start, depth)], held, sem)


def first_kernel(places, *refs):
    blocks, (weight, out, held, sems) = refs[:-4], refs[-4:]
    branches = out.shape[0]
    copies = [[fetch_rows(weight, j, owner(*p), held.at[j, k], sems.at[j, k]) for k, p in enumerate(places)] for j in range(branches)]
    for row in copies:
        for copy in row:
            copy.start()
    for j in range(branches):
        total = None
        for k in range(len(places)):
            copies[j][k].wait()
            term = jnp.dot(blocks[k][...], held[j, k], preferred_element_type=jnp.float32)
            total = term if total is None else total + term
        out[j] = total


def first_round(blocks, places, weight):
    branches, _, width = weight.shape
    rows, depth = blocks[0].shape
    count = len(blocks)
    return pl.pallas_call(
        functools.partial(first_kernel, places),
        out_shape=jax.ShapeDtypeStruct((branches, rows, width), jnp.float32),
        in_specs=[whole()] * count + [in_hbm()],
        out_specs=whole(),
        scratch_shapes=[pltpu.VMEM((branches, count, depth, width), jnp.bfloat16), pltpu.SemaphoreType.DMA((branches, count))],
        compiler_params=params(10), name="first_round",
        cost_estimate=pl.CostEstimate(flops=2 * count * rows * depth * branches * width, bytes_accessed=2 * count * depth * branches * width, transcendentals=0),
    )(*blocks, from_hbm(weight))


def signal_kernel(place, acc, lo, hi, halo, halo_acc, weight, taps, signal_t, signal, gate_out, sig_t, sig, gate, out_sems):
    branches, rows, width = acc.shape
    lead = halo.shape[0]
    block = jnp.concatenate([lo[...], hi[...]], axis=0)
    cols = 256
    outs = []
    for c in range(0, width, cols):
        short = []
        for j in range(branches):
            w = rows_of(weight, j, place, block.shape[1])[:, c:c + cols]
            here = acc[j, :, c:c + cols] + jnp.dot(block, w, preferred_element_type=jnp.float32)
            before = halo_acc[j, :, c:c + cols] + jnp.dot(halo[...], w, preferred_element_type=jnp.float32)
            here, before = [p.astype(jnp.bfloat16).astype(jnp.float32) for p in (here, before)]
            ext = jnp.concatenate([before, here], axis=0)
            tap = [taps[k, j:j + 1, c:c + cols] for k in range(3)]
            short.append(tap[0] * ext[lead - 2:lead - 2 + rows] + tap[1] * ext[lead - 1:lead - 1 + rows] + tap[2] * here)
        s = short[2] * short[1]
        k = c // cols
        sig_t[c:c + cols, :] = s.T.astype(jnp.bfloat16)
        sig[k] = s
        gate[k] = short[0]
        pairs = ((sig_t.at[c:c + cols, :], signal_t.at[c:c + cols, :]), (sig.at[k], signal.at[:, c:c + cols]), (gate.at[k], gate_out.at[:, c:c + cols]))
        for i, (src, dst) in enumerate(pairs):
            outs.append(pltpu.make_async_copy(src, dst, out_sems.at[i, k]))
            outs[-1].start()
    for copy in outs:
        copy.wait()


def signal_of(acc, lo, hi, halo, halo_acc, place, weight, taps):
    branches, rows, width = acc.shape
    depth = lo.shape[1]
    parts = width // 256
    return pl.pallas_call(
        functools.partial(signal_kernel, place),
        out_shape=[pltpu.HBM((width, rows), jnp.bfloat16)] + [pltpu.HBM((rows, width), jnp.float32)] * 2,
        in_specs=[whole()] * 7,
        out_specs=[in_hbm()] * 3,
        scratch_shapes=[
            pltpu.VMEM((width, rows), jnp.bfloat16),
            pltpu.VMEM((parts, rows, 256), jnp.float32),
            pltpu.VMEM((parts, rows, 256), jnp.float32),
            pltpu.SemaphoreType.DMA((3, parts)),
        ],
        compiler_params=params(12), name="signal_of",
        cost_estimate=pl.CostEstimate(flops=2 * rows * depth * branches * width, bytes_accessed=16 * rows * width, transcendentals=0),
    )(acc, lo, hi, halo, halo_acc, in_vmem(weight), taps)


def fetch_columns(weight, at, held, sem):
    cols = held.shape[1]
    start = pl.multiple_of(at * cols, cols)
    return pltpu.make_async_copy(weight.at[:, pl.ds(start, cols)], held, sem)


def gate_kernel(place, conv, signal, gate_out, skip, weight, gated, *refs):
    outs, (held, sem) = refs[:-2], refs[-2:]
    copy = fetch_columns(weight, owner(*place), held, sem)
    copy.start()
    total = conv[...].astype(jnp.float32).T + skip[...] * signal[...]
    g = (total * gate_out[...]).astype(jnp.bfloat16)
    gated[...] = g
    copy.wait()
    at = 0
    for out in outs:
        out[...] = jnp.dot(g[at:at + out.shape[0]], held[...], preferred_element_type=jnp.float32).astype(jnp.bfloat16)
        at += out.shape[0]


def gate_and_project(conv, signal, gate_out, skip, place, pieces, weight, cols):
    rows, width = signal.shape
    return pl.pallas_call(
        functools.partial(gate_kernel, place),
        out_shape=[jax.ShapeDtypeStruct((rows, width), jnp.bfloat16)] + [jax.ShapeDtypeStruct((n, cols), jnp.bfloat16) for n in pieces],
        in_specs=[whole()] * 4 + [in_hbm()],
        out_specs=[whole()] * (1 + len(pieces)),
        scratch_shapes=[pltpu.VMEM((width, cols), jnp.bfloat16), pltpu.SemaphoreType.DMA],
        compiler_params=params(10), name="gate_and_project",
        cost_estimate=pl.CostEstimate(flops=2 * rows * width * cols, bytes_accessed=12 * rows * width, transcendentals=0),
    )(conv, signal, gate_out, skip, weight)


def out_kernel(places, pieces, g, weight, *refs):
    count = len(places)
    outs, (held, sems) = list(refs[:sum(pieces)]), refs[sum(pieces):]
    copies = [fetch_columns(weight, owner(*p), held.at[k], sems.at[k]) for k, p in enumerate(places)]
    for copy in copies:
        copy.start()
    for k in range(count):
        copies[k].wait()
        for p in range(pieces[k]):
            out = outs.pop(0)
            part = out.shape[0]
            out[...] = jnp.dot(g[p * part:(p + 1) * part], held[k], preferred_element_type=jnp.float32).astype(jnp.bfloat16)


def project_out(gated, places, pieces, weight, cols):
    rows, width = gated.shape
    count = len(places)
    return pl.pallas_call(
        functools.partial(out_kernel, places, pieces),
        out_shape=[jax.ShapeDtypeStruct((rows // n, cols), jnp.bfloat16) for n in pieces for _ in range(n)],
        in_specs=[whole(), in_hbm()],
        out_specs=[whole()] * sum(pieces),
        scratch_shapes=[pltpu.VMEM((count, width, cols), jnp.bfloat16), pltpu.SemaphoreType.DMA((count,))],
        compiler_params=params(10), name="project_out",
        cost_estimate=pl.CostEstimate(flops=2 * count * rows * width * cols, bytes_accessed=4 * count * width * cols, transcendentals=0),
    )(gated, weight)


def added(*terms):
    return sum(t.astype(jnp.float32) for t in terms).astype(jnp.bfloat16)


def shards(tables, tokens, in_weight, short_weight, long_filter, skip_gain, out_weight):
    count = lax.axis_size("chan")
    seqs = lax.axis_size("seq")
    rows, width = tokens.shape
    half = rows // 2
    cols = out_weight.shape[1] // count
    weight = jnp.transpose(in_weight, (1, 0, 2))
    together = lax.optimization_barrier

    above, side, below = ring(tokens, -1), cross(tokens), ring(tokens, 1)
    halo = following_far(tokens[rows - 16:])
    above, side, below, halo, fil = together((above, side, below, halo, transposed(long_filter)))
    far, side_above, side_below = ring(above, -1), cross(above), ring(side, 1)
    fil = lax.all_to_all(fil, "seq", 0, 0, tiled=True)
    acc = first_round([tokens, below, above, side], [(0, 0), (-1, 0), (1, 0), (0, 1)], weight)
    far, side_above, side_below, acc = together((far, side_above, side_below, acc))
    far_hi, far_lo = ring(side_above[half:], -1), ring(side_below[:half], 1)
    acc, tail = project_round(acc, [side_below, side_above, far], [(-1, 1), (1, 1), (2, 0)], weight, 16)
    halo_acc = shifted(tail, "seq", 1)
    signal_t, signal, gate_out = signal_of(acc, far_lo, far_hi, halo, halo_acc, (2, 1), weight, short_weight)
    spec = filter_spectrum(fil, tables, seqs)

    conv = convolve(lax.all_to_all(signal_t, "seq", 0, 0, tiled=True), spec, tables, seqs)
    conv = lax.all_to_all(conv, "seq", 0, 0, tiled=True)

    skip = skip_gain.reshape(1, width)
    gated, to_far, to_up = gate_and_project(conv, signal, gate_out, skip, (2, 1), (half, half), out_weight, cols)
    to_far, to_up = cross(to_far), ring(to_up, 1)
    down_side, up_side, far = project_out(gated, [(-1, 1), (1, 1), (2, 0)], (1, 1, 1), out_weight, cols)
    down_side = ring(down_side, -1)
    up, down, side, own = project_out(gated, [(1, 0), (-1, 0), (0, 1), (0, 0)], (1, 1, 1, 1), out_weight, cols)
    up_side = cross(jnp.concatenate([up_side[:half], added(up_side[half:], to_up)], axis=0))
    far = ring(jnp.concatenate([added(far[:half], to_far), far[half:]], axis=0), 1)
    down_side, down = together((down_side, down))
    up_side, side = together((up_side, added(side, down_side)))
    side = cross(side)
    up = added(up, far, up_side)
    up, down = ring(up, 1), ring(down, -1)
    return added(own, down, side, up)


def solution(mesh):
    in_specs = (
        P("seq", "chan"),
        P(None, None, "chan"),
        P(None, None, "chan"),
        P("seq", "chan"),
        P("chan"),
        P("chan", None),
    )
    def run(*args):
        seqs = mesh.shape["seq"]
        tables = tuple(jnp.asarray(t) for t in fourier_tables(seqs, args[0].shape[0] // seqs))
        body = functools.partial(shards, tables)
        return jax.shard_map(body, mesh=mesh, in_specs=in_specs, out_specs=P("seq", "chan"), check_vma=False)(*args)
    return run
```

```python
import functools

import numpy as np
import jax
import jax.numpy as jnp
import ml_dtypes
from jax import lax
from jax.experimental import pallas as pl
from jax.experimental.pallas import tpu as pltpu
from jax.sharding import PartitionSpec as P

K1 = 72
GROUP = 32


def fourier_tables(seqs, rows):
    total = 2 * seqs * rows
    fine = 128
    coarse = total // fine
    half = coarse // 2
    per = rows // fine
    n1 = (np.arange(seqs)[None, :] * per + np.arange(per)[:, None]).reshape(-1)
    k1 = np.arange(half + 1)
    ang = 2 * np.pi * ((k1[:, None] * n1[None, :]) % coarse) / coarse
    pad = ((0, K1 - half - 1), (0, 0))
    first = np.concatenate([np.pad(np.cos(ang), pad), np.pad(-np.sin(ang), pad)])
    weight = np.where((k1 == 0) | (k1 == half), 1.0, 2.0)[:, None]
    last = np.concatenate([np.pad(weight * np.cos(ang), pad), np.pad(-weight * np.sin(ang), pad)]).T
    n2 = np.arange(fine)
    tw = 2 * np.pi * (k1[:, None] * n2[None, :]) / total
    tw_cos, tw_sin = np.pad(np.cos(tw), pad), np.pad(np.sin(tw), pad)
    ang2 = 2 * np.pi * ((n2[:, None] * n2[None, :]) % fine) / fine
    c, s = np.cos(ang2), np.sin(ang2)
    forward = np.block([[c, -s], [s, c]])
    backward = np.block([[c, s], [-s, c]])
    bf = ml_dtypes.bfloat16
    twiddle = np.stack([tw_cos, tw_sin]).astype(np.float32)
    return first.astype(bf), twiddle, forward.astype(bf), backward.astype(bf), last.astype(bf)


def spectrum_of(xs, base, seqs, chans, first, tw, forward):
    cols = []
    for i in range(GROUP):
        cols.append(jnp.concatenate([xs[p, pl.ds(base + i, seqs, stride=chans), :] for p in range(xs.shape[0])], axis=0))
    x = jnp.concatenate(cols, axis=1).astype(jnp.bfloat16)
    s = jnp.dot(first[...], x, preferred_element_type=jnp.float32)
    tc, ts = tw[0], tw[1]
    z = []
    for i in range(GROUP):
        re, im = s[:K1, i * 128:(i + 1) * 128], s[K1:, i * 128:(i + 1) * 128]
        z.append(jnp.concatenate([re * tc + im * ts, im * tc - re * ts], axis=1))
    z = jnp.concatenate(z, axis=0).astype(jnp.bfloat16)
    return jnp.dot(z, forward[...], preferred_element_type=jnp.float32)


def filter_kernel(seqs, chans, x_ref, first, tw, forward, out, xs, held, sems):
    for p in range(xs.shape[0]):
        xs[p] = x_ref[:, p * 128:(p + 1) * 128].astype(jnp.float32)

    @pl.loop(0, chans // GROUP)
    def _(g):
        held[g] = spectrum_of(xs, g * GROUP, seqs, chans, first, tw, forward).astype(jnp.bfloat16)
        pltpu.make_async_copy(held.at[g], out.at[g], sems.at[g]).start()

    @pl.loop(0, chans // GROUP)
    def _(g):
        pltpu.make_async_copy(held.at[g], out.at[g], sems.at[g]).wait()


def conv_kernel(seqs, chans, scale, x_ref, h_ref, first, tw, forward, backward, last, out, xs, ys, held, sems):
    for g in range(chans // GROUP):
        pltpu.make_async_copy(h_ref.at[g], held.at[g], sems.at[g]).start()
    for p in range(xs.shape[0]):
        xs[p] = x_ref[:, p * 128:(p + 1) * 128].astype(jnp.float32)

    @pl.loop(0, chans // GROUP)
    def _(g):
        q = spectrum_of(xs, g * GROUP, seqs, chans, first, tw, forward)
        pltpu.make_async_copy(h_ref.at[g], held.at[g], sems.at[g]).wait()
        h = held[g].astype(jnp.float32)
        qr, qi, hr, hi = q[:, :128], q[:, 128:], h[:, :128], h[:, 128:]
        p = jnp.concatenate([qr * hr - qi * hi, qr * hi + qi * hr], axis=1).astype(jnp.bfloat16)
        u = jnp.dot(p, backward[...], preferred_element_type=jnp.float32)
        tc, ts = tw[0] * scale, tw[1] * scale
        v = []
        for i in range(GROUP):
            re, im = u[i * K1:(i + 1) * K1, :128], u[i * K1:(i + 1) * K1, 128:]
            v.append(jnp.concatenate([re * tc - im * ts, im * tc + re * ts], axis=0))
        v = jnp.concatenate(v, axis=1).astype(jnp.bfloat16)
        y = jnp.dot(last[...], v, preferred_element_type=jnp.float32)
        for i in range(GROUP):
            yi = y[:, i * 128:(i + 1) * 128]
            for p in range(ys.shape[0]):
                ys[p, pl.ds(g * GROUP + i, seqs, stride=chans), :] = yi[p * seqs:(p + 1) * seqs]

    for p in range(ys.shape[0]):
        out[:, p * 128:(p + 1) * 128] = ys[p].astype(jnp.bfloat16)


def whole():
    return pl.BlockSpec(memory_space=pltpu.VMEM)

def params(mib):
    return pltpu.CompilerParams(vmem_limit_bytes=mib * 1024 * 1024)


def filter_spectrum(x, tables, seqs):
    chans = x.shape[0] // seqs
    first, tw, forward, _, _ = tables
    shape = (chans // GROUP, GROUP * K1, 256)
    return pl.pallas_call(
        functools.partial(filter_kernel, seqs, chans),
        out_shape=pltpu.HBM(shape, jnp.bfloat16),
        in_specs=[whole()] * 4, out_specs=in_hbm(),
        scratch_shapes=[
            pltpu.VMEM((x.shape[1] // 128, x.shape[0], 128), jnp.float32),
            pltpu.VMEM(shape, jnp.bfloat16),
            pltpu.SemaphoreType.DMA(shape[:1]),
        ],
        compiler_params=params(16),
        name="filter_spectrum",
        cost_estimate=pl.CostEstimate(flops=4_000_000_000, bytes_accessed=4_000_000, transcendentals=0),
    )(x, first, tw, forward)


def convolve(x, spec, tables, seqs):
    rows = x.shape[1]
    chans = x.shape[0] // seqs
    first, tw, forward, backward, last = tables
    return pl.pallas_call(
        functools.partial(conv_kernel, seqs, chans, 1.0 / (2 * seqs * rows)),
        out_shape=jax.ShapeDtypeStruct(x.shape, jnp.bfloat16),
        in_specs=[whole(), in_hbm()] + [whole()] * 5, out_specs=whole(),
        scratch_shapes=[pltpu.VMEM((x.shape[1] // 128, x.shape[0], 128), jnp.float32)] * 2
        + [pltpu.VMEM(spec.shape, spec.dtype), pltpu.SemaphoreType.DMA(spec.shape[:1])],
        compiler_params=params(20),
        name="convolve",
        cost_estimate=pl.CostEstimate(flops=5_000_000_000, bytes_accessed=4_000_000, transcendentals=0),
    )(x, from_hbm(spec), first, tw, forward, backward, last)


def shifted(array, axis, by):
    count = lax.axis_size(axis)
    pairs = [(i, i + by) for i in range(count) if 0 <= i + by < count]
    return lax.ppermute(array, axis, pairs)


def ring(array, by):
    count = lax.axis_size("chan")
    return lax.ppermute(array, "chan", [(i, (i + 2 * by) % count) for i in range(count)])


def cross(array):
    count = lax.axis_size("chan")
    return lax.ppermute(array, "chan", [(i, i ^ 1) for i in range(count)])


def following_far(array):
    seqs, count = lax.axis_size("seq"), lax.axis_size("chan")
    pairs = [(s * count + c, (s + 1) * count + (((c + 4) % count) ^ 1)) for s in range(seqs - 1) for c in range(count)]
    return lax.ppermute(array, ("seq", "chan"), pairs)


def transpose_kernel(x_ref, out):
    out[...] = x_ref[...].T.astype(jnp.bfloat16)


def transposed(x):
    return pl.pallas_call(
        transpose_kernel,
        out_shape=jax.ShapeDtypeStruct(x.shape[::-1], jnp.bfloat16),
        in_specs=[whole()], out_specs=whole(),
        compiler_params=params(8), name="transposed",
        cost_estimate=pl.CostEstimate(flops=0, bytes_accessed=6 * x.size, transcendentals=0),
    )(x)


def owner(dy, dx):
    count = lax.axis_size("chan")
    return jnp.bitwise_xor(lax.rem(lax.axis_index("chan") + 2 * (dy % (count // 2)), count), dx)


def from_hbm(array):
    return pltpu.with_memory_space_constraint(array, pltpu.HBM)


def in_hbm():
    return pl.BlockSpec(memory_space=pltpu.HBM)


def in_vmem(array):
    return pltpu.with_memory_space_constraint(array, pltpu.VMEM)


def rows_of(weight, j, place, depth):
    start = pl.multiple_of(owner(*place) * depth, depth)
    return weight[j, pl.ds(start, depth), :]


def round_kernel(places, has_acc, tail, *refs):
    refs = list(refs)
    acc = refs.pop(0) if has_acc else None
    blocks = [refs.pop(0) for _ in places]
    weight, out, *tail_out = refs
    for j in range(out.shape[0]):
        total = acc[j] if has_acc else None
        for block, place in zip(blocks, places):
            term = jnp.dot(block[...], rows_of(weight, j, place, block.shape[1]), preferred_element_type=jnp.float32)
            total = term if total is None else total + term
        out[j] = total
        if tail:
            tail_out[0][j] = total[total.shape[0] - tail:]


def project_round(acc, blocks, places, weight, tail=0):
    branches, _, width = weight.shape
    rows, depth = blocks[0].shape
    count = len(blocks)
    args = ([acc] if acc is not None else []) + blocks
    return pl.pallas_call(
        functools.partial(round_kernel, places, acc is not None, tail),
        out_shape=[jax.ShapeDtypeStruct((branches, n, width), jnp.float32) for n in ((rows, tail) if tail else (rows,))],
        in_specs=[whole()] * (len(args) + 1),
        out_specs=[whole()] * (2 if tail else 1),
        compiler_params=params(10), name="project_round",
        cost_estimate=pl.CostEstimate(flops=2 * count * rows * depth * branches * width, bytes_accessed=2 * count * depth * branches * width, transcendentals=0),
    )(*args, in_vmem(weight))


def fetch_rows(weight, j, at, held, sem):
    depth = held.shape[0]
    start = pl.multiple_of(at * depth, depth)
    return pltpu.make_async_copy(weight.at[j, pl.ds(start, depth)], held, sem)


def first_kernel(places, *refs):
    blocks, (weight, out, held, sems) = refs[:-4], refs[-4:]
    branches = out.shape[0]
    copies = [[fetch_rows(weight, j, owner(*p), held.at[j, k], sems.at[j, k]) for k, p in enumerate(places)] for j in range(branches)]
    for row in copies:
        for copy in row:
            copy.start()
    for j in range(branches):
        total = None
        for k in range(len(places)):
            copies[j][k].wait()
            term = jnp.dot(blocks[k][...], held[j, k], preferred_element_type=jnp.float32)
            total = term if total is None else total + term
        out[j] = total


def first_round(blocks, places, weight):
    branches, _, width = weight.shape
    rows, depth = blocks[0].shape
    count = len(blocks)
    return pl.pallas_call(
        functools.partial(first_kernel, places),
        out_shape=jax.ShapeDtypeStruct((branches, rows, width), jnp.float32),
        in_specs=[whole()] * count + [in_hbm()],
        out_specs=whole(),
        scratch_shapes=[pltpu.VMEM((branches, count, depth, width), jnp.bfloat16), pltpu.SemaphoreType.DMA((branches, count))],
        compiler_params=params(10), name="first_round",
        cost_estimate=pl.CostEstimate(flops=2 * count * rows * depth * branches * width, bytes_accessed=2 * count * depth * branches * width, transcendentals=0),
    )(*blocks, from_hbm(weight))


def signal_kernel(place, acc, lo, hi, halo, halo_acc, weight, taps, signal_t, signal, gate_out, sig_t, sig, gate, out_sems):
    branches, rows, width = acc.shape
    lead = halo.shape[0]
    block = jnp.concatenate([lo[...], hi[...]], axis=0)
    cols = 256
    outs = []
    for c in range(0, width, cols):
        short = []
        for j in range(branches):
            w = rows_of(weight, j, place, block.shape[1])[:, c:c + cols]
            here = acc[j, :, c:c + cols] + jnp.dot(block, w, preferred_element_type=jnp.float32)
            before = halo_acc[j, :, c:c + cols] + jnp.dot(halo[...], w, preferred_element_type=jnp.float32)
            here, before = [p.astype(jnp.bfloat16).astype(jnp.float32) for p in (here, before)]
            ext = jnp.concatenate([before, here], axis=0)
            tap = [taps[k, j:j + 1, c:c + cols] for k in range(3)]
            short.append(tap[0] * ext[lead - 2:lead - 2 + rows] + tap[1] * ext[lead - 1:lead - 1 + rows] + tap[2] * here)
        s = short[2] * short[1]
        k = c // cols
        sig_t[c:c + cols, :] = s.T.astype(jnp.bfloat16)
        sig[k] = s
        gate[k] = short[0]
        pairs = ((sig_t.at[c:c + cols, :], signal_t.at[c:c + cols, :]), (sig.at[k], signal.at[:, c:c + cols]), (gate.at[k], gate_out.at[:, c:c + cols]))
        for i, (src, dst) in enumerate(pairs):
            outs.append(pltpu.make_async_copy(src, dst, out_sems.at[i, k]))
            outs[-1].start()
    for copy in outs:
        copy.wait()


def signal_of(acc, lo, hi, halo, halo_acc, place, weight, taps):
    branches, rows, width = acc.shape
    depth = lo.shape[1]
    parts = width // 256
    return pl.pallas_call(
        functools.partial(signal_kernel, place),
        out_shape=[pltpu.HBM((width, rows), jnp.bfloat16)] + [pltpu.HBM((rows, width), jnp.float32)] * 2,
        in_specs=[whole()] * 7,
        out_specs=[in_hbm()] * 3,
        scratch_shapes=[
            pltpu.VMEM((width, rows), jnp.bfloat16),
            pltpu.VMEM((parts, rows, 256), jnp.float32),
            pltpu.VMEM((parts, rows, 256), jnp.float32),
            pltpu.SemaphoreType.DMA((3, parts)),
        ],
        compiler_params=params(12), name="signal_of",
        cost_estimate=pl.CostEstimate(flops=2 * rows * depth * branches * width, bytes_accessed=16 * rows * width, transcendentals=0),
    )(acc, lo, hi, halo, halo_acc, in_vmem(weight), taps)


def fetch_columns(weight, at, held, sem):
    cols = held.shape[1]
    start = pl.multiple_of(at * cols, cols)
    return pltpu.make_async_copy(weight.at[:, pl.ds(start, cols)], held, sem)


def gate_kernel(place, conv, signal, gate_out, skip, weight, gated, *refs):
    outs, (held, sem) = refs[:-2], refs[-2:]
    copy = fetch_columns(weight, owner(*place), held, sem)
    copy.start()
    total = conv[...].astype(jnp.float32).T + skip[...] * signal[...]
    g = (total * gate_out[...]).astype(jnp.bfloat16)
    gated[...] = g
    copy.wait()
    at = 0
    for out in outs:
        out[...] = jnp.dot(g[at:at + out.shape[0]], held[...], preferred_element_type=jnp.float32).astype(jnp.bfloat16)
        at += out.shape[0]


def gate_and_project(conv, signal, gate_out, skip, place, pieces, weight, cols):
    rows, width = signal.shape
    return pl.pallas_call(
        functools.partial(gate_kernel, place),
        out_shape=[jax.ShapeDtypeStruct((rows, width), jnp.bfloat16)] + [jax.ShapeDtypeStruct((n, cols), jnp.bfloat16) for n in pieces],
        in_specs=[whole()] * 4 + [in_hbm()],
        out_specs=[whole()] * (1 + len(pieces)),
        scratch_shapes=[pltpu.VMEM((width, cols), jnp.bfloat16), pltpu.SemaphoreType.DMA],
        compiler_params=params(10), name="gate_and_project",
        cost_estimate=pl.CostEstimate(flops=2 * rows * width * cols, bytes_accessed=12 * rows * width, transcendentals=0),
    )(conv, signal, gate_out, skip, weight)


def out_kernel(places, pieces, g, weight, *refs):
    count = len(places)
    outs, (held, sems) = list(refs[:sum(pieces)]), refs[sum(pieces):]
    copies = [fetch_columns(weight, owner(*p), held.at[k], sems.at[k]) for k, p in enumerate(places)]
    for copy in copies:
        copy.start()
    for k in range(count):
        copies[k].wait()
        for p in range(pieces[k]):
            out = outs.pop(0)
            part = out.shape[0]
            out[...] = jnp.dot(g[p * part:(p + 1) * part], held[k], preferred_element_type=jnp.float32).astype(jnp.bfloat16)


def project_out(gated, places, pieces, weight, cols):
    rows, width = gated.shape
    count = len(places)
    return pl.pallas_call(
        functools.partial(out_kernel, places, pieces),
        out_shape=[jax.ShapeDtypeStruct((rows // n, cols), jnp.bfloat16) for n in pieces for _ in range(n)],
        in_specs=[whole(), in_hbm()],
        out_specs=[whole()] * sum(pieces),
        scratch_shapes=[pltpu.VMEM((count, width, cols), jnp.bfloat16), pltpu.SemaphoreType.DMA((count,))],
        compiler_params=params(10), name="project_out",
        cost_estimate=pl.CostEstimate(flops=2 * count * rows * width * cols, bytes_accessed=4 * count * width * cols, transcendentals=0),
    )(gated, weight)


def added(*terms):
    return sum(t.astype(jnp.float32) for t in terms).astype(jnp.bfloat16)


def shards(tables, tokens, in_weight, short_weight, long_filter, skip_gain, out_weight):
    count = lax.axis_size("chan")
    seqs = lax.axis_size("seq")
    rows, width = tokens.shape
    half = rows // 2
    cols = out_weight.shape[1] // count
    weight = jnp.transpose(in_weight, (1, 0, 2))
    together = lax.optimization_barrier

    above, side, below = ring(tokens, -1), cross(tokens), ring(tokens, 1)
    halo = following_far(tokens[rows - 16:])
    above, side, below, halo, fil = together((above, side, below, halo, transposed(long_filter)))
    far, side_above, side_below = ring(above, -1), cross(above), ring(side, 1)
    fil = lax.all_to_all(fil, "seq", 0, 0, tiled=True)
    acc = first_round([tokens, below, above, side], [(0, 0), (-1, 0), (1, 0), (0, 1)], weight)
    far, side_above, side_below, acc = together((far, side_above, side_below, acc))
    far_hi, far_lo = ring(side_above[half:], -1), ring(side_below[:half], 1)
    acc, tail = project_round(acc, [side_below, side_above, far], [(-1, 1), (1, 1), (2, 0)], weight, 16)
    halo_acc = shifted(tail, "seq", 1)
    signal_t, signal, gate_out = signal_of(acc, far_lo, far_hi, halo, halo_acc, (2, 1), weight, short_weight)
    spec = filter_spectrum(fil, tables, seqs)

    conv = convolve(lax.all_to_all(signal_t, "seq", 0, 0, tiled=True), spec, tables, seqs)
    conv = lax.all_to_all(conv, "seq", 0, 0, tiled=True)

    skip = skip_gain.reshape(1, width)
    gated, to_far, to_up = gate_and_project(conv, signal, gate_out, skip, (2, 1), (half, half), out_weight, cols)
    to_far, to_up = cross(to_far), ring(to_up, 1)
    down_side, up_side, far = project_out(gated, [(-1, 1), (1, 1), (2, 0)], (1, 1, 1), out_weight, cols)
    to_up, down_side = together((to_up, down_side))
    down_side = ring(down_side, -1)
    up, down, side, own = project_out(gated, [(1, 0), (-1, 0), (0, 1), (0, 0)], (1, 1, 1, 1), out_weight, cols)
    up_side = cross(jnp.concatenate([up_side[:half], added(up_side[half:], to_up)], axis=0))
    far = ring(jnp.concatenate([added(far[:half], to_far), far[half:]], axis=0), 1)
    down_side, down = together((down_side, down))
    up_side, own = together((up_side, own))
    side = added(side, down_side)
    side = cross(side)
    up = added(up, far, up_side)
    up, down = ring(up, 1), ring(down, -1)
    return added(own, down, side, up)


def solution(mesh):
    in_specs = (
        P("seq", "chan"),
        P(None, None, "chan"),
        P(None, None, "chan"),
        P("seq", "chan"),
        P("chan"),
        P("chan", None),
    )
    def run(*args):
        seqs = mesh.shape["seq"]
        tables = tuple(jnp.asarray(t) for t in fourier_tables(seqs, args[0].shape[0] // seqs))
        body = functools.partial(shards, tables)
        return jax.shard_map(body, mesh=mesh, in_specs=in_specs, out_specs=P("seq", "chan"), check_vma=False)(*args)
    return run
```
